32 devices in a mesh: dp: 4 (over y, x), ctx: 8 (over z, core).
Axes of the slice: x: 2, y: 2, z: 4, core: 2. Of those that a mesh axis runs over, the one named last changes fastest.
Arguments:
- query: bfloat16 [4, 1024, 4096], P('dp', 'ctx'), may hold values from -5 to 5
- keys: bfloat16 [4, 1024, 512], P('dp', 'ctx'), may hold values from -5 to 5
- values: bfloat16 [4, 1024, 512], P('dp', 'ctx'), may hold values from -6 to 6
- out_grad: bfloat16 [4, 1024, 4096], P('dp', 'ctx'), may hold values from -16 to 16
- query_lowrank_state: bfloat16 [4, 1024, 8], P('dp', 'ctx'), may hold values from -0.25 to 0.25
- value_lowrank_state: bfloat16 [4, 1024, 8], P('dp', 'ctx'), may hold values from -0.25 to 0.25
- shift_flags: int32 [4], replicated, may hold values from 0 to 1, as said below
Outputs:
- query_gradient: bfloat16 [4, 1024, 4096], P('dp', 'ctx')
- key_gradient: bfloat16 [4, 1024, 512], P('dp', 'ctx')
- value_gradient: bfloat16 [4, 1024, 512], P('dp', 'ctx')
- query_adapter_gradient: float32 [8, 4096], replicated
- value_adapter_gradient: float32 [8, 512], replicated
The draws below stay inside these ranges and needn't reach their ends.
Inputs may be any that keep to these rules, and one draw needn't show every extreme that they name: `shift_flags`: exactly half of the 4 entries are 1, the others 0.
All inputs are finite; a program needn't handle non-finite values.
Results may differ from the reference program's by a relative error of at most 0.012.
Values may be sent and summed in bfloat16 or wider, within the bound.
A program may use at most 64 MiB of HBM per device.

```python
import math
import jax
import jax.numpy as jnp
from jax import lax

QUERY_HEADS_HALF = 32
KEY_VALUE_HEADS = 4
HEAD_WIDTH = 128
ADAPTER_RANK = 8
TOK_DEV = 128
GROUP_DEV = 8
BATCH = 4
SEQ = 1024
DEVICES = 32


def draw_query(key, part):
    key = jax.random.fold_in(key, 3)
    array_shape = (BATCH, SEQ, KEY_VALUE_HEADS, QUERY_HEADS_HALF // KEY_VALUE_HEADS, HEAD_WIDTH)
    drawn_rows = jax.random.truncated_normal(key, -5.0, 5.0, array_shape, jnp.float32)
    return drawn_rows.reshape(BATCH, SEQ, QUERY_HEADS_HALF * HEAD_WIDTH).astype(jnp.bfloat16)


def draw_keys(key, part):
    key = jax.random.fold_in(key, 5)
    array_shape = (BATCH, SEQ, KEY_VALUE_HEADS, 1, HEAD_WIDTH)
    drawn_rows = jax.random.truncated_normal(key, -5.0, 5.0, array_shape, jnp.float32)
    return drawn_rows.reshape(BATCH, SEQ, KEY_VALUE_HEADS * HEAD_WIDTH).astype(jnp.bfloat16)


def draw_shift_flags(key, part):
    key = jax.random.fold_in(key, 7)
    shuffled = jax.random.permutation(key, KEY_VALUE_HEADS)
    return (shuffled < KEY_VALUE_HEADS // 2).astype(jnp.int32)


def block_levels(key, shape, pieces, low, top_value):
    def one(dim, shards_of):
        heights = jax.random.uniform(jax.random.fold_in(jax.random.fold_in(key, 6), dim), (shards_of,), jnp.float32, low / len(pieces), top_value / len(pieces))
        return jnp.repeat(jnp.exp(heights), shape[dim] // shards_of).reshape((-1,) + (1,) * (len(shape) - dim - 1))

    gain = one(*pieces[0])
    for cut in pieces[1:]:
        gain = gain * one(*cut)
    return gain


def centred(key, dims, scale, limit, shards=(), held_as=jnp.bfloat16):
    result = scale * jax.random.normal(key, dims, jnp.float32)
    if shards:
        result = result * block_levels(key, dims, shards, -0.22, 0.18)
    return jnp.clip(result, -limit, limit).astype(held_as)


def setup_inputs(seed: int = 0) -> dict:
    key_list = jax.random.split(jax.random.key(seed), 8)
    return {
        "query": draw_query(jax.random.fold_in(key_list[7], 71), 0),
        "keys": draw_keys(jax.random.fold_in(key_list[7], 71), 0),
        "values": centred(key_list[2], (BATCH, SEQ, KEY_VALUE_HEADS * HEAD_WIDTH), 1.0, 6.0, ((0, 4), (1, 8))),
        "out_grad": centred(key_list[3], (BATCH, SEQ, QUERY_HEADS_HALF * HEAD_WIDTH), 4.0, 16.0, ((0, 4), (1, 8))),
        "query_lowrank_state": centred(key_list[4], (BATCH, SEQ, ADAPTER_RANK), (3.0 / (TOK_DEV * DEVICES) ** 0.5), 0.25, ((0, 4), (1, 8))),
        "value_lowrank_state": centred(key_list[5], (BATCH, SEQ, ADAPTER_RANK), (3.0 / (TOK_DEV * DEVICES) ** 0.5), 0.25, ((0, 4), (1, 8))),
        "shift_flags": draw_shift_flags(jax.random.fold_in(key_list[7], 71), 0),
    }


ADAPTER_SCALE = 2.0

def rope_back(gradient, positions):
    half_dim = gradient.shape[-1] // 2
    inv_freq = 10000.0 ** (-(jnp.arange(half_dim, dtype=jnp.float32) * 2.0) / gradient.shape[-1])
    angles = positions.astype(jnp.float32)[:, None] * inv_freq[None, :]
    table_shape = (angles.shape[0],) + (1,) * (gradient.ndim - 2) + (half_dim,)
    cosine = jnp.cos(angles).reshape(table_shape)
    sine_table = jnp.sin(angles).reshape(table_shape)
    front_half = gradient[..., :half_dim]
    back_half = gradient[..., half_dim:]
    return jnp.concatenate([front_half * cosine + back_half * sine_table, back_half * cosine - front_half * sine_table], axis=-1)

def head_backward(operands):
    q_seq, k_seq, v_seq, d_seq, flag_value = operands
    group_len = TOK_DEV * GROUP_DEV
    half_len = group_len // 2
    n_groups = SEQ // group_len
    shifted = flag_value == 1

    def arrange(tensor):
        return jnp.where(shifted, jnp.roll(tensor, -half_len, axis=0), tensor)
    q_grp = arrange(q_seq).astype(jnp.float32).reshape(n_groups, group_len, -1, HEAD_WIDTH)
    d_grp = arrange(d_seq).astype(jnp.float32).reshape(n_groups, group_len, -1, HEAD_WIDTH)
    k_grp = arrange(k_seq).astype(jnp.float32).reshape(n_groups, group_len, HEAD_WIDTH)
    v_grp = arrange(v_seq).astype(jnp.float32).reshape(n_groups, group_len, HEAD_WIDTH)
    score_scale = 1.0 / math.sqrt(HEAD_WIDTH)
    causal = jnp.arange(group_len)[:, None] >= jnp.arange(group_len)[None, :]
    raw_score = jnp.einsum('nqgd,nkd->ngqk', q_grp, k_grp) * score_scale
    raw_score = jnp.where(causal, raw_score, -jnp.inf)
    log_total = jax.nn.logsumexp(raw_score, axis=-1, keepdims=True)
    probs = jnp.exp(raw_score - log_total)
    dprob = jnp.einsum('nqgd,nkd->ngqk', d_grp, v_grp)
    delta_row = lax.optimization_barrier(jnp.sum(probs * dprob, axis=-1, keepdims=True))
    dscore = probs * (dprob - delta_row)
    prob_low = lax.optimization_barrier(probs.astype(jnp.bfloat16)).astype(jnp.float32)
    dscore_low = lax.optimization_barrier(dscore.astype(jnp.bfloat16)).astype(jnp.float32)
    dq_grp = jnp.einsum('ngqk,nkd->nqgd', dscore_low, k_grp) * score_scale
    dk_grp = jnp.einsum('ngqk,nqgd->nkd', dscore_low, q_grp) * score_scale
    dv_grp = jnp.einsum('ngqk,nqgd->nkd', prob_low, d_grp)

    def restore(tensor):
        flat_rows = tensor.reshape((SEQ,) + tensor.shape[2:])
        return jnp.where(shifted, jnp.roll(flat_rows, half_len, axis=0), flat_rows)
    return (restore(dq_grp), restore(dk_grp), restore(dv_grp))

def reference(query, keys, values, out_grad, query_lowrank_state, value_lowrank_state, shift_flags):
    per_group = QUERY_HEADS_HALF // KEY_VALUE_HEADS

    def by_head(tensor, per_head):
        shaped = tensor.reshape((BATCH, SEQ, KEY_VALUE_HEADS) + per_head)
        return jnp.moveaxis(shaped, 2, 1).reshape((BATCH * KEY_VALUE_HEADS, SEQ) + per_head)

    def back_layout(tensor, per_head):
        shaped = tensor.reshape((BATCH, KEY_VALUE_HEADS, SEQ) + per_head)
        return jnp.moveaxis(shaped, 1, 2)
    flag_items = jnp.tile(shift_flags, BATCH).astype(jnp.int32)
    dq_all, dk_all, dv_all = lax.map(head_backward, (by_head(query, (per_group, HEAD_WIDTH)), by_head(keys, (HEAD_WIDTH,)), by_head(values, (HEAD_WIDTH,)), by_head(out_grad, (per_group, HEAD_WIDTH)), flag_items))
    positions = jnp.arange(SEQ, dtype=jnp.int32)
    dq_full = back_layout(dq_all, (per_group, HEAD_WIDTH))
    dk_full = back_layout(dk_all, (HEAD_WIDTH,))
    dv_full = back_layout(dv_all, (HEAD_WIDTH,))
    query_gradient = jax.vmap(lambda gradient: rope_back(gradient, positions))(dq_full).astype(jnp.bfloat16).reshape(BATCH, SEQ, QUERY_HEADS_HALF * HEAD_WIDTH)
    key_gradient = jax.vmap(lambda gradient: rope_back(gradient, positions))(dk_full).astype(jnp.bfloat16).reshape(BATCH, SEQ, KEY_VALUE_HEADS * HEAD_WIDTH)
    value_gradient = dv_full.astype(jnp.bfloat16).reshape(BATCH, SEQ, KEY_VALUE_HEADS * HEAD_WIDTH)
    query_adapter_gradient = ADAPTER_SCALE * jnp.dot(query_lowrank_state.reshape(-1, ADAPTER_RANK).T, query_gradient.reshape(-1, QUERY_HEADS_HALF * HEAD_WIDTH), preferred_element_type=jnp.float32)
    value_adapter_gradient = ADAPTER_SCALE * jnp.dot(value_lowrank_state.reshape(-1, ADAPTER_RANK).T, value_gradient.reshape(-1, KEY_VALUE_HEADS * HEAD_WIDTH), preferred_element_type=jnp.float32)
    return (query_gradient, key_gradient, value_gradient, query_adapter_gradient, value_adapter_gradient)
```

```python
import functools
import math

import jax
import jax.numpy as jnp
from jax import lax
from jax.experimental import pallas as pl
from jax.experimental.pallas import tpu as pltpu
from jax.sharding import PartitionSpec as P

KV_HEADS = 4
PER_GROUP = 8
WIDTH = 128
TOK = 128
GROUP_CHIPS = 4
SPAN = PER_GROUP * WIDTH
ADAPTER_SCALE = 2.0
SCORE_SCALE = 1.0 / math.sqrt(WIDTH)
EXP2_SCALE = SCORE_SCALE * math.log2(math.e)
MESH = pl.DeviceIdType.MESH
F32 = jnp.float32
BF16 = jnp.bfloat16


def arrange_kernel(order, q, d, k, v, q_out, d_out, kv_out):
    q_out[0] = q[...]
    d_out[0] = d[...]
    kv_out[0, 0] = k[...]
    kv_out[0, 1] = v[...]


def arrange(order, q, d, k, v):
    spec = pltpu.PrefetchScalarGridSpec(
        num_scalar_prefetch=1,
        grid=(KV_HEADS,),
        in_specs=[
            pl.BlockSpec((TOK, SPAN), lambda s, o: (0, o[s])),
            pl.BlockSpec((TOK, SPAN), lambda s, o: (0, o[s])),
            pl.BlockSpec((TOK, WIDTH), lambda s, o: (0, o[s])),
            pl.BlockSpec((TOK, WIDTH), lambda s, o: (0, o[s])),
        ],
        out_specs=[
            pl.BlockSpec((1, TOK, SPAN), lambda s, o: (s, 0, 0)),
            pl.BlockSpec((1, TOK, SPAN), lambda s, o: (s, 0, 0)),
            pl.BlockSpec((1, 2, TOK, WIDTH), lambda s, o: (s, 0, 0, 0)),
        ],
    )
    return pl.pallas_call(
        arrange_kernel,
        grid_spec=spec,
        out_shape=[
            jax.ShapeDtypeStruct((KV_HEADS, TOK, SPAN), BF16),
            jax.ShapeDtypeStruct((KV_HEADS, TOK, SPAN), BF16),
            jax.ShapeDtypeStruct((KV_HEADS, 2, TOK, WIDTH), BF16),
        ],
        name="arrange_heads",
    )(order, q, d, k, v)


def restore_kernel(place, q, k, v, qa, va, q_out, k_out, v_out, qa_out, va_out):
    q_out[...] = q[0]
    k_out[...] = k[0]
    v_out[...] = v[0]
    qa_out[...] = qa[...]
    va_out[...] = va[...]


def restore(place, q, k, v, qa, va):
    wide = pl.BlockSpec((1, TOK, SPAN), lambda h, p: (p[h], 0, 0))
    narrow = pl.BlockSpec((1, TOK, WIDTH), lambda h, p: (p[h], 0, 0))
    spec = pltpu.PrefetchScalarGridSpec(
        num_scalar_prefetch=1,
        grid=(KV_HEADS,),
        in_specs=[
            wide,
            narrow,
            narrow,
            pl.BlockSpec((8, SPAN), lambda h, p: (0, p[h])),
            pl.BlockSpec((8, WIDTH), lambda h, p: (0, p[h])),
        ],
        out_specs=[
            pl.BlockSpec((TOK, SPAN), lambda h, p: (0, h)),
            pl.BlockSpec((TOK, WIDTH), lambda h, p: (0, h)),
            pl.BlockSpec((TOK, WIDTH), lambda h, p: (0, h)),
            pl.BlockSpec((8, SPAN), lambda h, p: (0, h)),
            pl.BlockSpec((8, WIDTH), lambda h, p: (0, h)),
        ],
    )
    return pl.pallas_call(
        restore_kernel,
        grid_spec=spec,
        out_shape=[
            jax.ShapeDtypeStruct((TOK, KV_HEADS * SPAN), BF16),
            jax.ShapeDtypeStruct((TOK, KV_HEADS * WIDTH), BF16),
            jax.ShapeDtypeStruct((TOK, KV_HEADS * WIDTH), BF16),
            jax.ShapeDtypeStruct((8, KV_HEADS * SPAN), F32),
            jax.ShapeDtypeStruct((8, KV_HEADS * WIDTH), F32),
        ],
        name="restore_heads",
    )(place, q, k, v, qa, va)


def dot(a, b, dims):
    return lax.dot_general(a, b, (dims, ((), ())), preferred_element_type=F32)


NT = ((1,), (1,))
NN = ((1,), (0,))


def attend(nb, us, pair, core_unused, qb, db, kvb, kT, cosT, sinT, acc, dqb):
    cols = [pl.ds(pl.multiple_of(pair * 2 * WIDTH + g * WIDTH, WIDTH), WIDTH) for g in range(2)]
    rows_q = jnp.concatenate([qb[us, h, :, cols[g]] for g in range(2) for h in range(2)], axis=0)
    rows_d = jnp.concatenate([db[us, h, :, cols[g]] for g in range(2) for h in range(2)], axis=0)
    n_rows = 4 * TOK
    score = []
    dprob = []
    for t in range(nb):
        key = kvb[us, t, :, 0].reshape(2 * TOK, WIDTH)
        val = kvb[us, t, :, 1].reshape(2 * TOK, WIDTH)
        s = dot(key, rows_q, NT)
        if t == 0:
            kpos = lax.broadcasted_iota(jnp.int32, (2 * TOK, n_rows), 0)
            rpos = lax.broadcasted_iota(jnp.int32, (2 * TOK, n_rows), 1) & (2 * TOK - 1)
            s = jnp.where(kpos <= rpos, s, -jnp.inf)
        score.append(s)
        dprob.append(dot(val, rows_d, NT))
    top = functools.reduce(jnp.maximum, [jnp.max(s, axis=0, keepdims=True) for s in score])
    weight = [jnp.exp2((s - top) * EXP2_SCALE) for s in score]
    total = sum(jnp.sum(w, axis=0, keepdims=True) for w in weight)
    mixed = sum(jnp.sum(w * dp, axis=0, keepdims=True) for w, dp in zip(weight, dprob))
    inverse = 1.0 / total
    delta = mixed * inverse
    dqT = jnp.zeros((WIDTH, n_rows), F32)
    for t in range(nb):
        prob = weight[t] * inverse
        ds = (prob * (dprob[t] - delta)).astype(BF16)
        acc[t, 1] += dot(prob.astype(BF16), rows_d, NN)
        acc[t, 0] += dot(ds, rows_q, NN)
        dqT = dqT + dot(kT[t], ds, NN)
    cos = cosT[...]
    sin = sinT[...]
    cos = jnp.concatenate([cos, cos], axis=1)
    sin = jnp.concatenate([sin, sin], axis=1)
    front = dqT[: WIDTH // 2] * SCORE_SCALE
    back = dqT[WIDTH // 2 :] * SCORE_SCALE
    turned = jnp.concatenate([front * cos + back * sin, back * cos - front * sin], axis=0)
    dq = turned.T.astype(BF16)
    for g in range(2):
        for h in range(2):
            at = (g * 2 + h) * TOK
            dqb[us, h, :, cols[g]] = dq[at : at + TOK]


def main_kernel(
    n, ndp,
    q, d, kv, st, cosT, sinT, cosF, sinF,
    qg, kg, vg, qa, va,
    qb, db, kvb, stb, kT, acc, psend, rbuf, dqb, own,
    qap, qzr, qds, qdr, qas, vap, vzr, vds, vdr,
    kvs, kvr, qs, qr, ss, sr, ps, pr, dqs, dqr,
    qzs_s, qzr_s, qds_s, qdr_s, qas_s, qar_s, vzs_s, vzr_s, vds_s, vdr_s,
):
    nz = n // 2
    wide = 2 * SPAN // nz
    me = lax.axis_index("ctx")
    dpi = lax.axis_index("dp")
    z = me // 2
    c = me % 2
    other = 1 - c
    sib = z * 2 + other

    def slot(us, zz):
        return (zz + 2 * us) % GROUP_CHIPS

    def copy(src, dst, send, recv, target):
        return pltpu.make_async_remote_copy(
            src_ref=src, dst_ref=dst, send_sem=send, recv_sem=recv,
            device_id=target, device_id_type=MESH,
        )

    barrier = pltpu.get_barrier_semaphore()

    @pl.loop(1, n)
    def _(o):
        pl.semaphore_signal(barrier, inc=1, device_id=(dpi, (me + o) % n), device_id_type=MESH)

    @pl.loop(1, ndp)
    def _(o):
        pl.semaphore_signal(barrier, inc=1, device_id=((dpi + o) % ndp, me), device_id_type=MESH)

    pl.semaphore_wait(barrier, n - 1 + ndp - 1)

    def near_kv(us):
        return copy(kv.at[2 * other + us], kvb.at[us, 0, c], kvs.at[us, 0, other], kvr.at[us, 0, c], (dpi, sib))

    def far_kv(us, t, cc):
        zt = (z + t) % nz
        return copy(kv.at[2 * cc + us], kvb.at[us, t, c], kvs.at[us, t, cc], kvr.at[us, t, c], (dpi, 2 * zt + cc))

    def near_rows(us, i):
        src, dst = ((q, qb), (d, db))[i]
        return copy(src.at[2 * other + us], dst.at[us, c], qs.at[us, i], qr.at[us, i], (dpi, sib))

    def near_state():
        return copy(st, stb.at[c], ss, sr, (dpi, sib))

    def far_part(us, t, h):
        zo = (z - t + nz) % nz
        return copy(psend.at[us, t, h], rbuf.at[us, t, c], ps.at[us, t, h], pr.at[us, t, c], (dpi, 2 * zo + h))

    def near_part(us):
        return copy(psend.at[us, 0, other], rbuf.at[us, 0, c], ps.at[us, 0, other], pr.at[us, 0, c], (dpi, sib))

    def near_dq(us):
        return copy(dqb.at[us, other], qg.at[2 * c + us], dqs.at[us], dqr.at[us], (dpi, sib))

    early = (z // 2) % 2

    @pl.loop(0, 2)
    def _(step):
        us = (step + early) % 2
        near_rows(us, 0).start()
        near_kv(us).start()
        near_rows(us, 1).start()

        @pl.loop(1, GROUP_CHIPS)
        def _(t):
            @pl.when(t <= slot(us, (z + t) % nz))
            def _():
                far_kv(us, t, 0).start()
                far_kv(us, t, 1).start()

    near_state().start()
    stb[c] = st[...]

    @pl.loop(0, 2)
    def _(us):
        qb[us, c] = q[2 * c + us]
        db[us, c] = d[2 * c + us]
        kvb[us, 0, c] = kv[2 * c + us]

    @pl.loop(0, 2)
    def _(step):
        us = (step + early) % 2
        nb = slot(us, z) + 1
        copy(kv.at[0], kvb.at[us, 0, other], kvs.at[us, 0, other], kvr.at[us, 0, other], (dpi, sib)).wait_recv()
        near_rows(us, 0).wait_recv()
        near_rows(us, 1).wait_recv()

        @pl.loop(1, nb)
        def _(t):
            for h in range(2):
                copy(kv.at[0], kvb.at[us, t, h], kvs.at[us, t, h], kvr.at[us, t, h], (dpi, sib)).wait_recv()

        @pl.loop(0, nb)
        def _(t):
            kT[t] = kvb[us, t, :, 0].reshape(2 * TOK, WIDTH).astype(F32).T.astype(BF16)
            acc[t] = jnp.zeros((2, 2 * TOK, WIDTH), F32)

        for count in range(1, GROUP_CHIPS + 1):
            @pl.when(nb == count)
            def _(count=count):
                @pl.loop(0, PER_GROUP // 2)
                def _(pair):
                    attend(count, us, pair, c, qb, db, kvb, kT, cosT, sinT, acc, dqb)

        @pl.loop(0, nb)
        def _(t):
            for h in range(2):
                psend[us, t, h] = acc[t, :, h * TOK : (h + 1) * TOK].astype(BF16)

        @pl.loop(1, nb)
        def _(t):
            far_part(us, t, 0).start()
            far_part(us, t, 1).start()

        near_part(us).start()
        near_dq(us).start()
        rbuf[us, 0, c] = psend[us, 0, c]
        qg[2 * c + us] = dqb[us, c]

        @pl.when(step == 0)
        def _():
            copy(st, stb.at[other], ss, sr, (dpi, sib)).wait_recv()

        part = dot(stb[0], dqb[us, 0], NN) + dot(stb[1], dqb[us, 1], NN)
        for j in range(nz // 2):
            qap[us * (nz // 2) + j] = part[:8, j * wide : (j + 1) * wide]

    def qz(k):
        return copy(qap.at[k], qzr.at[z], qzs_s.at[k], qzr_s.at[z], (dpi, 2 * k + c))

    @pl.loop(1, nz)
    def _(o):
        qz((z + o) % nz).start()

    qzr[z] = qap[z]

    @pl.loop(0, 2)
    def _(step):
        us = (step + early) % 2
        copy(kv.at[0], rbuf.at[us, 0, other], ps.at[us, 0, other], pr.at[us, 0, other], (dpi, sib)).wait_recv()
        for cc in range(2):
            own[us, cc] = rbuf[us, 0, cc].astype(F32)

        @pl.loop(1, GROUP_CHIPS)
        def _(t):
            @pl.when(t <= slot(us, (z + t) % nz))
            def _():
                for cc in range(2):
                    copy(kv.at[0], rbuf.at[us, t, cc], ps.at[us, t, cc], pr.at[us, t, cc], (dpi, sib)).wait_recv()
                    own[us, cc] += rbuf[us, t, cc].astype(F32)

    for cc in range(2):
        for us in range(2):
            place = 2 * cc + us
            dk = own[us, cc, 0] * SCORE_SCALE
            kg[place] = (dk * cosF[...] + pltpu.roll(dk, WIDTH // 2, 1) * sinF[...]).astype(BF16)
            dv = own[us, cc, 1].astype(BF16)
            vg[place] = dv
            vap[:, place * WIDTH : (place + 1) * WIDTH] = dot(st[...], dv, NN)[8:]

    def vz(o):
        return copy(vap, vzr.at[me], vzs_s.at[o], vzr_s.at[me], (dpi, (me + o) % n))

    @pl.loop(1, n)
    def _(o):
        vz(o).start()

    vzr[me] = vap[...]

    @pl.loop(1, nz)
    def _(o):
        k = (z + o) % nz
        copy(qap.at[k], qzr.at[k], qzs_s.at[k], qzr_s.at[k], (dpi, sib)).wait_recv()

    qds[...] = lax.fori_loop(0, nz, lambda k, x: x + qzr[k], jnp.zeros((8, wide), F32))

    def qd(o):
        return copy(qds, qdr.at[dpi], qds_s.at[o], qdr_s.at[dpi], ((dpi + o) % ndp, me))

    @pl.loop(1, ndp)
    def _(o):
        qd(o).start()

    qdr[dpi] = qds[...]

    @pl.loop(1, n)
    def _(o):
        k = (me + o) % n
        copy(vap, vzr.at[k], vzs_s.at[o], vzr_s.at[k], (dpi, sib)).wait_recv()

    vds[...] = lax.fori_loop(0, n, lambda k, x: x + vzr[k], jnp.zeros((8, KV_HEADS * WIDTH), F32))

    def vd(o):
        return copy(vds, vdr.at[dpi], vds_s.at[o], vdr_s.at[dpi], ((dpi + o) % ndp, me))

    @pl.loop(1, ndp)
    def _(o):
        vd(o).start()

    vdr[dpi] = vds[...]

    @pl.loop(1, ndp)
    def _(o):
        k = (dpi + o) % ndp
        copy(qds, qdr.at[k], qds_s.at[o], qdr_s.at[k], (dpi, sib)).wait_recv()

    qas[...] = lax.fori_loop(0, ndp, lambda k, x: x + qdr[k], jnp.zeros((8, wide), F32)) * ADAPTER_SCALE

    def qag(o):
        return copy(qas, qa.at[me], qas_s.at[o], qar_s.at[me], (dpi, (me + o) % n))

    @pl.loop(1, n)
    def _(o):
        qag(o).start()

    qa[me] = qas[...]

    @pl.loop(1, ndp)
    def _(o):
        k = (dpi + o) % ndp
        copy(vds, vdr.at[k], vds_s.at[o], vdr_s.at[k], (dpi, sib)).wait_recv()

    va[...] = (
        lax.fori_loop(0, ndp, lambda k, x: x + vdr[k], jnp.zeros((8, KV_HEADS * WIDTH), F32)) * ADAPTER_SCALE
    )

    @pl.loop(0, 2)
    def _(us):
        copy(dqb.at[us, other], qg.at[2 * other + us], dqs.at[us], dqr.at[us], (dpi, sib)).wait_recv()
        near_dq(us).wait_send()
        near_kv(us).wait_send()
        near_rows(us, 0).wait_send()
        near_rows(us, 1).wait_send()
        near_part(us).wait_send()

        @pl.loop(1, GROUP_CHIPS)
        def _(t):
            @pl.when(t <= slot(us, (z + t) % nz))
            def _():
                far_kv(us, t, 0).wait_send()
                far_kv(us, t, 1).wait_send()

            @pl.when(t <= slot(us, z))
            def _():
                far_part(us, t, 0).wait_send()
                far_part(us, t, 1).wait_send()

    near_state().wait_send()

    @pl.loop(1, nz)
    def _(o):
        qz((z + o) % nz).wait_send()

    @pl.loop(1, ndp)
    def _(o):
        qd(o).wait_send()
        vd(o).wait_send()

    @pl.loop(1, n)
    def _(o):
        vz(o).wait_send()
        qag(o).wait_send()
        k = (me + o) % n
        copy(qas, qa.at[k], qas_s.at[o], qar_s.at[k], (dpi, sib)).wait_recv()


def main_call(n, ndp, *operands):
    nz = n // 2
    wide = 2 * SPAN // nz
    vmem = pl.BlockSpec(memory_space=pltpu.VMEM)
    dma = pltpu.SemaphoreType.DMA
    hw = KV_HEADS * WIDTH
    return pl.pallas_call(
        functools.partial(main_kernel, n, ndp),
        in_specs=[vmem] * len(operands),
        out_specs=[vmem] * 5,
        out_shape=[
            jax.ShapeDtypeStruct((KV_HEADS, TOK, SPAN), BF16),
            jax.ShapeDtypeStruct((KV_HEADS, TOK, WIDTH), BF16),
            jax.ShapeDtypeStruct((KV_HEADS, TOK, WIDTH), BF16),
            jax.ShapeDtypeStruct((n, 8, wide), F32),
            jax.ShapeDtypeStruct((8, hw), F32),
        ],
        scratch_shapes=[
            pltpu.VMEM((2, 2, TOK, SPAN), BF16),
            pltpu.VMEM((2, 2, TOK, SPAN), BF16),
            pltpu.VMEM((2, GROUP_CHIPS, 2, 2, TOK, WIDTH), BF16),
            pltpu.VMEM((2, 16, TOK), BF16),
            pltpu.VMEM((GROUP_CHIPS, WIDTH, 2 * TOK), BF16),
            pltpu.VMEM((GROUP_CHIPS, 2, 2 * TOK, WIDTH), F32),
            pltpu.VMEM((2, GROUP_CHIPS, 2, 2, TOK, WIDTH), BF16),
            pltpu.VMEM((2, GROUP_CHIPS, 2, 2, TOK, WIDTH), BF16),
            pltpu.VMEM((2, 2, TOK, SPAN), BF16),
            pltpu.VMEM((2, 2, 2, TOK, WIDTH), F32),
            pltpu.VMEM((nz, 8, wide), F32),
            pltpu.VMEM((nz, 8, wide), F32),
            pltpu.VMEM((8, wide), F32),
            pltpu.VMEM((ndp, 8, wide), F32),
            pltpu.VMEM((8, wide), F32),
            pltpu.VMEM((8, hw), F32),
            pltpu.VMEM((n, 8, hw), F32),
            pltpu.VMEM((8, hw), F32),
            pltpu.VMEM((ndp, 8, hw), F32),
            dma((2, GROUP_CHIPS, 2)), dma((2, GROUP_CHIPS, 2)),
            dma((2, 2)), dma((2, 2)),
            dma, dma,
            dma((2, GROUP_CHIPS, 2)), dma((2, GROUP_CHIPS, 2)),
            dma((2,)), dma((2,)),
            dma((nz,)), dma((nz,)),
            dma((ndp,)), dma((ndp,)),
            dma((n,)), dma((n,)),
            dma((n,)), dma((n,)),
            dma((ndp,)), dma((ndp,)),
        ],
        compiler_params=pltpu.CompilerParams(
            collective_id=0, has_side_effects=True, vmem_limit_bytes=56 * 1024 * 1024
        ),
        name="attention_backward",
    )(*operands)


def local(n, ndp, query, keys, values, out_grad, query_state, value_state, flags):
    nz = n // 2
    wide = 2 * SPAN // nz
    me = lax.axis_index("ctx")
    z = me // 2
    heads = jnp.arange(KV_HEADS, dtype=jnp.int32)
    before = heads[None, :] < heads[:, None]
    same = flags[None, :] == flags[:, None]
    place = 2 * jnp.sum(before & same, axis=1, dtype=jnp.int32) + flags
    order = jnp.sum(jnp.where(place[None, :] == heads[:, None], heads[None, :], 0), axis=1, dtype=jnp.int32)

    half = WIDTH // 2
    inv_freq = 10000.0 ** (-(jnp.arange(half, dtype=F32) * 2.0) / WIDTH)
    chip_pos = (z * 2 * TOK + jnp.arange(2 * TOK, dtype=jnp.int32)).astype(F32)
    angleT = inv_freq[:, None] * chip_pos[None, :]
    cosT = jnp.cos(angleT)
    sinT = jnp.sin(angleT)
    cos_own = lax.dynamic_slice(cosT, (0, (me % 2) * TOK), (half, TOK)).T
    sin_own = lax.dynamic_slice(sinT, (0, (me % 2) * TOK), (half, TOK)).T
    cosF = jnp.concatenate([cos_own, cos_own], axis=1)
    sinF = jnp.concatenate([sin_own, -sin_own], axis=1)
    state = jnp.concatenate([query_state[0], value_state[0]], axis=1).T

    q4, d4, kv4 = arrange(order, query[0], out_grad[0], keys[0], values[0])
    qg, kg, vg, qa, va = main_call(n, ndp, q4, d4, kv4, state, cosT, sinT, cosF, sinF)
    qa = qa.reshape(nz, 2, 8, wide).transpose(2, 1, 0, 3).reshape(8, KV_HEADS * SPAN)
    qg, kg, vg, qa, va = restore(place, qg, kg, vg, qa, va)
    return qg[None], kg[None], vg[None], qa, va


def solution(mesh):
    split = P("dp", "ctx", None)
    return jax.shard_map(
        functools.partial(local, mesh.shape["ctx"], mesh.shape["dp"]),
        mesh=mesh,
        in_specs=(split,) * 6 + (P(),),
        out_specs=(split, split, split, P(), P()),
        check_vma=False,
    )
```

```python
import functools
import math

import jax
import jax.numpy as jnp
from jax import lax
from jax.experimental import pallas as pl
from jax.experimental.pallas import tpu as pltpu
from jax.sharding import PartitionSpec as P
import numpy as np

KV_HEADS = 4
PER_GROUP = 8
WIDTH = 128
TOK = 128
GROUP_CHIPS = 4
SPAN = PER_GROUP * WIDTH
ADAPTER_SCALE = 2.0
SCORE_SCALE = 1.0 / math.sqrt(WIDTH)
EXP2_SCALE = SCORE_SCALE * math.log2(math.e)
MESH = pl.DeviceIdType.MESH
F32 = jnp.float32
BF16 = jnp.bfloat16


def dot(a, b, dims):
    return lax.dot_general(a, b, (dims, ((), ())), preferred_element_type=F32)


NT = ((1,), (1,))
NN = ((1,), (0,))


def attend(nb, us, pair, qb, db, kvb, kT, table, acc, dqb):
    span = nb * 2 * TOK
    cols = [pl.ds(pl.multiple_of(pair * 2 * WIDTH + g * WIDTH, WIDTH), WIDTH) for g in range(2)]
    rows_q = jnp.concatenate([qb[us, h, :, cols[g]] for g in range(2) for h in range(2)], axis=0)
    rows_d = jnp.concatenate([db[us, h, :, cols[g]] for g in range(2) for h in range(2)], axis=0)
    n_rows = 4 * TOK
    key = kvb[us, 0:nb, :, 0].reshape(span, WIDTH)
    val = kvb[us, 0:nb, :, 1].reshape(span, WIDTH)
    score = dot(key, rows_q, NT)
    kpos = lax.broadcasted_iota(jnp.int32, (2 * TOK, n_rows), 0)
    rpos = lax.broadcasted_iota(jnp.int32, (2 * TOK, n_rows), 1) & (2 * TOK - 1)
    diagonal = jnp.where(kpos <= rpos, score[: 2 * TOK], -jnp.inf)
    score = diagonal if nb == 1 else jnp.concatenate([diagonal, score[2 * TOK :]], axis=0)
    dprob = dot(val, rows_d, NT)
    top = jnp.max(score, axis=0, keepdims=True)
    weight = jnp.exp2((score - top) * EXP2_SCALE)
    total = jnp.sum(weight, axis=0, keepdims=True)
    mixed = jnp.sum(weight * dprob, axis=0, keepdims=True)
    inverse = 1.0 / total
    delta = mixed * inverse
    prob = weight * inverse
    ds = (prob * (dprob - delta)).astype(BF16)
    acc[1, :span] += dot(prob.astype(BF16), rows_d, NN)
    acc[0, :span] += dot(ds, rows_q, NN)
    dqT = dot(kT[:, :span], ds, NN)
    cos = jnp.concatenate([table[0], table[0]], axis=1)
    sin = jnp.concatenate([table[1], table[1]], axis=1)
    front = dqT[: WIDTH // 2] * SCORE_SCALE
    back = dqT[WIDTH // 2 :] * SCORE_SCALE
    turned = jnp.concatenate([front * cos + back * sin, back * cos - front * sin], axis=0)
    dq = turned.T.astype(BF16)
    for g in range(2):
        for h in range(2):
            at = (g * 2 + h) * TOK
            dqb[us, h, :, cols[g]] = dq[at : at + TOK]


def main_kernel(
    n, ndp,
    flags, q_hbm, d_hbm, k_in, v_in, sq, sv, tables,
    qg, kg, vg, qa, va,
    q, d, table, qsend, dsend, kv,
    qb, db, kvb, st, stb, kT, acc, psend, rbuf, dqb, qgs, own,
    vpart, msg, zr, zsum, dr, res, gat,
    loads, kvs, kvr, qs, qr, ss, sr, ps, pr, dqs, dqr,
    zs_s, zr_s, ds_s, dr_s, as_s, ar_s,
):
    nz = n // 2
    wide = 2 * SPAN // nz
    me = lax.axis_index("ctx")
    dpi = lax.axis_index("dp")
    z = me // 2
    c = me % 2
    other = 1 - c
    sib = z * 2 + other

    def slot(us, zz):
        return (zz + 2 * us) % GROUP_CHIPS

    def copy(src, dst, send, recv, target):
        return pltpu.make_async_remote_copy(
            src_ref=src, dst_ref=dst, send_sem=send, recv_sem=recv,
            device_id=target, device_id_type=MESH,
        )

    load_q = pltpu.make_async_copy(q_hbm, q, loads.at[0])
    load_d = pltpu.make_async_copy(d_hbm, d, loads.at[1])
    load_t = pltpu.make_async_copy(tables.at[z], table, loads.at[2])
    load_q.start()
    load_d.start()
    load_t.start()

    barrier = pltpu.get_barrier_semaphore()

    @pl.loop(1, n)
    def _(o):
        pl.semaphore_signal(barrier, inc=1, device_id=(dpi, (me + o) % n), device_id_type=MESH)

    @pl.loop(1, ndp)
    def _(o):
        pl.semaphore_signal(barrier, inc=1, device_id=((dpi + o) % ndp, me), device_id_type=MESH)

    flag = [flags[h] for h in range(KV_HEADS)]

    def same(a, b):
        return 1 - (a - b) * (a - b)

    rank = [sum((same(flag[j], flag[h]) for j in range(h)), jnp.int32(0)) for h in range(KV_HEADS)]

    def share(h, cc, us):
        return (same(rank[h], cc) * same(flag[h], us)).astype(F32)

    def pick(parts, weights):
        total = None
        for part, weight in zip(parts, weights):
            term = part * jnp.full(part.shape, weight, F32).astype(part.dtype)
            total = term if total is None else total + term
        return total

    def gather(ref, width, cc, us):
        heads = range(KV_HEADS)
        return pick([ref[:, h * width : (h + 1) * width] for h in heads], [share(h, cc, us) for h in heads])

    st[...] = jnp.concatenate([sq[...].astype(F32), sv[...].astype(F32)], axis=0).astype(BF16)
    stb[0, c] = st[...]
    for s in range(KV_HEADS):
        kv[s, 0] = gather(k_in, WIDTH, s // 2, s % 2)
        kv[s, 1] = gather(v_in, WIDTH, s // 2, s % 2)
    early = (z // 2) % 2
    load_q.wait()
    load_d.wait()
    for us in range(2):
        qsend[us] = gather(q, SPAN, other, us)
        dsend[us] = gather(d, SPAN, other, us)
        qb[us, c] = gather(q, SPAN, c, us)
        db[us, c] = gather(d, SPAN, c, us)
        kvb[us, 0, c] = kv[2 * c + us]
    load_t.wait()

    pl.semaphore_wait(barrier, n - 1 + ndp - 1)

    def near_kv(us):
        return copy(kv.at[2 * other + us], kvb.at[us, 0, c], kvs.at[us, 0, other], kvr.at[us, 0, c], (dpi, sib))

    def far_kv(us, t, cc):
        zt = (z + t) % nz
        return copy(kv.at[2 * cc + us], kvb.at[us, t, c], kvs.at[us, t, cc], kvr.at[us, t, c], (dpi, 2 * zt + cc))

    def near_rows(us, i):
        src, dst = ((qsend, qb), (dsend, db))[i]
        return copy(src.at[us], dst.at[us, c], qs.at[us, i], qr.at[us, i], (dpi, sib))

    def near_state():
        return copy(st, stb.at[0, c], ss.at[0, other], sr.at[0, c], (dpi, sib))

    def far_state(t, cc):
        zt = (z + t) % nz
        return copy(st, stb.at[t, c], ss.at[t, cc], sr.at[t, c], (dpi, 2 * zt + cc))

    def far_part(us, t, h):
        zo = (z - t + nz) % nz
        return copy(psend.at[us, t, h], rbuf.at[us, t, c], ps.at[us, t, h], pr.at[us, t, c], (dpi, 2 * zo + h))

    def near_part(us):
        return copy(psend.at[us, 0, other], rbuf.at[us, 0, c], ps.at[us, 0, other], pr.at[us, 0, c], (dpi, sib))

    def near_dq(us):
        return copy(dqb.at[us, other], qgs.at[2 * c + us], dqs.at[us], dqr.at[us], (dpi, sib))

    @pl.loop(0, 2)
    def _(step):
        us = (step + early) % 2
        near_kv(us).start()
        near_rows(us, 0).start()
        near_rows(us, 1).start()

        @pl.loop(1, GROUP_CHIPS)
        def _(t):
            @pl.when(t <= slot(us, (z + t) % nz))
            def _():
                far_kv(us, t, 0).start()
                far_kv(us, t, 1).start()

    near_state().start()

    @pl.loop(1, GROUP_CHIPS)
    def _(t):
        far_state(t, 0).start()
        far_state(t, 1).start()

    @pl.loop(0, 2)
    def _(step):
        us = (step + early) % 2
        nb = slot(us, z) + 1
        copy(kv.at[0], kvb.at[us, 0, other], kvs.at[us, 0, other], kvr.at[us, 0, other], (dpi, sib)).wait_recv()
        near_rows(us, 0).wait_recv()
        near_rows(us, 1).wait_recv()

        @pl.loop(1, nb)
        def _(t):
            for h in range(2):
                copy(kv.at[0], kvb.at[us, t, h], kvs.at[us, t, h], kvr.at[us, t, h], (dpi, sib)).wait_recv()

        @pl.loop(0, nb)
        def _(t):
            at = pl.ds(pl.multiple_of(t * 2 * TOK, 2 * TOK), 2 * TOK)
            kT[:, at] = kvb[us, t, :, 0].reshape(2 * TOK, WIDTH).astype(F32).T.astype(BF16)
            acc[0, at] = jnp.zeros((2 * TOK, WIDTH), F32)
            acc[1, at] = jnp.zeros((2 * TOK, WIDTH), F32)

        for count in range(1, GROUP_CHIPS + 1):
            @pl.when(nb == count)
            def _(count=count):
                @pl.loop(0, PER_GROUP // 2)
                def _(pair):
                    attend(count, us, pair, qb, db, kvb, kT, table, acc, dqb)

        near_dq(us).start()

        @pl.loop(0, nb)
        def _(t):
            for h in range(2):
                at = pl.ds(pl.multiple_of(t * 2 * TOK + h * TOK, TOK), TOK)
                psend[us, t, h, 0] = acc[0, at].astype(BF16)
                psend[us, t, h, 1] = acc[1, at].astype(BF16)

            @pl.when(t > 0)
            def _():
                far_part(us, t, 0).start()
                far_part(us, t, 1).start()

        near_part(us).start()

        @pl.when(step == 0)
        def _():
            copy(st, stb.at[0, other], ss.at[0, other], sr.at[0, other], (dpi, sib)).wait_recv()

            @pl.loop(1, GROUP_CHIPS)
            def _(t):
                for h in range(2):
                    copy(st, stb.at[t, h], ss.at[t, h], sr.at[t, h], (dpi, sib)).wait_recv()

        part = dot(stb[0, 0], dqb[us, 0], NN) + dot(stb[0, 1], dqb[us, 1], NN)
        for j in range(nz // 2):
            msg[us * (nz // 2) + j, :, :wide] = part[:8, j * wide : (j + 1) * wide]

        def value_term(t, x):
            return x + dot(stb[t, 0], psend[us, t, 0, 1], NN) + dot(stb[t, 1], psend[us, t, 1, 1], NN)

        vpart[us] = lax.fori_loop(0, nb, value_term, jnp.zeros((16, WIDTH), F32))
        rbuf[us, 0, c] = psend[us, 0, c]
        qgs[2 * c + us] = dqb[us, c]

    for k in range(nz):
        for us in range(2):
            msg[k, :, wide + us * WIDTH : wide + (us + 1) * WIDTH] = vpart[us, 8:]

    def to_chip(k):
        return copy(msg.at[k], zr.at[z], zs_s.at[k], zr_s.at[z], (dpi, 2 * k + c))

    @pl.loop(1, nz)
    def _(o):
        to_chip((z + o) % nz).start()

    zr[z] = msg[z]

    @pl.loop(1, nz)
    def _(o):
        k = (z + o) % nz
        copy(msg.at[k], zr.at[k], zs_s.at[k], zr_s.at[k], (dpi, sib)).wait_recv()

    zsum[...] = lax.fori_loop(0, nz, lambda k, x: x + zr[k], jnp.zeros((8, wide + 2 * WIDTH), F32))

    def to_dp(o):
        return copy(zsum, dr.at[dpi], ds_s.at[o], dr_s.at[dpi], ((dpi + o) % ndp, me))

    @pl.loop(1, ndp)
    def _(o):
        to_dp(o).start()

    dr[dpi] = zsum[...]

    def owner_sum(us):
        copy(kv.at[0], rbuf.at[us, 0, other], ps.at[us, 0, other], pr.at[us, 0, other], (dpi, sib)).wait_recv()
        for cc in range(2):
            own[us, cc] = rbuf[us, 0, cc].astype(F32)

        @pl.loop(1, GROUP_CHIPS)
        def _(t):
            @pl.when(t <= slot(us, (z + t) % nz))
            def _():
                for cc in range(2):
                    copy(kv.at[0], rbuf.at[us, t, cc], ps.at[us, t, cc], pr.at[us, t, cc], (dpi, sib)).wait_recv()
                    own[us, cc] += rbuf[us, t, cc].astype(F32)

    @pl.loop(1, ndp)
    def _(o):
        k = (dpi + o) % ndp
        copy(zsum, dr.at[k], ds_s.at[o], dr_s.at[k], (dpi, sib)).wait_recv()

    res[...] = (
        lax.fori_loop(0, ndp, lambda k, x: x + dr[k], jnp.zeros((8, wide + 2 * WIDTH), F32)) * ADAPTER_SCALE
    )

    def to_ctx(o):
        return copy(res, gat.at[me], as_s.at[o], ar_s.at[me], (dpi, (me + o) % n))

    @pl.loop(1, n)
    def _(o):
        to_ctx(o).start()

    gat[me] = res[...]

    def spread(h):
        return [share(h, s // 2, s % 2) for s in range(KV_HEADS)]

    @pl.loop(0, 2)
    def _(us):
        copy(dqb.at[us, other], qgs.at[2 * other + us], dqs.at[us], dqr.at[us], (dpi, sib)).wait_recv()

    for h in range(KV_HEADS):
        qg[:, h * SPAN : (h + 1) * SPAN] = pick([qgs[s] for s in range(KV_HEADS)], spread(h))

    @pl.loop(0, 2)
    def _(us):
        owner_sum(us)

    cos = jnp.where(c == 0, table[0, :, :TOK], table[0, :, TOK:]).T
    sin = jnp.where(c == 0, table[1, :, :TOK], table[1, :, TOK:]).T
    cos = jnp.concatenate([cos, cos], axis=1)
    sin = jnp.concatenate([sin, -sin], axis=1)
    for h in range(KV_HEADS):
        at = slice(h * WIDTH, (h + 1) * WIDTH)
        dk = pick([own[s % 2, s // 2, 0] for s in range(KV_HEADS)], spread(h)) * SCORE_SCALE
        kg[:, at] = (dk * cos + pltpu.roll(dk, WIDTH // 2, 1) * sin).astype(BF16)
        vg[:, at] = pick([own[s % 2, s // 2, 1] for s in range(KV_HEADS)], spread(h)).astype(BF16)

    @pl.loop(1, n)
    def _(o):
        k = (me + o) % n
        copy(res, gat.at[k], as_s.at[o], ar_s.at[k], (dpi, sib)).wait_recv()

    for h in range(KV_HEADS):
        for j in range(nz // 2):
            at = h * SPAN + j * wide
            held = [gat[2 * (s % 2 * (nz // 2) + j) + s // 2, :, :wide] for s in range(KV_HEADS)]
            qa[:, at : at + wide] = pick(held, spread(h))
        held = [gat[s // 2, :, wide + s % 2 * WIDTH : wide + (s % 2 + 1) * WIDTH] for s in range(KV_HEADS)]
        va[:, h * WIDTH : (h + 1) * WIDTH] = pick(held, spread(h))

    @pl.loop(0, 2)
    def _(us):
        near_dq(us).wait_send()
        near_kv(us).wait_send()
        near_rows(us, 0).wait_send()
        near_rows(us, 1).wait_send()
        near_part(us).wait_send()

        @pl.loop(1, GROUP_CHIPS)
        def _(t):
            @pl.when(t <= slot(us, (z + t) % nz))
            def _():
                far_kv(us, t, 0).wait_send()
                far_kv(us, t, 1).wait_send()

            @pl.when(t <= slot(us, z))
            def _():
                far_part(us, t, 0).wait_send()
                far_part(us, t, 1).wait_send()

    near_state().wait_send()

    @pl.loop(1, GROUP_CHIPS)
    def _(t):
        far_state(t, 0).wait_send()
        far_state(t, 1).wait_send()

    @pl.loop(1, nz)
    def _(o):
        to_chip((z + o) % nz).wait_send()

    @pl.loop(1, ndp)
    def _(o):
        to_dp(o).wait_send()

    @pl.loop(1, n)
    def _(o):
        to_ctx(o).wait_send()


def main_call(n, ndp, *operands):
    nz = n // 2
    line = 2 * SPAN // nz + 2 * WIDTH
    vmem = pl.BlockSpec(memory_space=pltpu.VMEM)
    smem = pl.BlockSpec(memory_space=pltpu.SMEM)
    away = pl.BlockSpec(memory_space=pl.ANY)
    dma = pltpu.SemaphoreType.DMA
    hw = KV_HEADS * WIDTH
    return pl.pallas_call(
        functools.partial(main_kernel, n, ndp),
        in_specs=[smem, away, away, vmem, vmem, vmem, vmem, away],
        out_specs=[vmem] * 5,
        out_shape=[
            jax.ShapeDtypeStruct((TOK, KV_HEADS * SPAN), BF16),
            jax.ShapeDtypeStruct((TOK, hw), BF16),
            jax.ShapeDtypeStruct((TOK, hw), BF16),
            jax.ShapeDtypeStruct((8, KV_HEADS * SPAN), F32),
            jax.ShapeDtypeStruct((8, hw), F32),
        ],
        scratch_shapes=[
            pltpu.VMEM((TOK, KV_HEADS * SPAN), BF16),
            pltpu.VMEM((TOK, KV_HEADS * SPAN), BF16),
            pltpu.VMEM((2, WIDTH // 2, 2 * TOK), F32),
            pltpu.VMEM((2, TOK, SPAN), BF16),
            pltpu.VMEM((2, TOK, SPAN), BF16),
            pltpu.VMEM((KV_HEADS, 2, TOK, WIDTH), BF16),
            pltpu.VMEM((2, 2, TOK, SPAN), BF16),
            pltpu.VMEM((2, 2, TOK, SPAN), BF16),
            pltpu.VMEM((2, GROUP_CHIPS, 2, 2, TOK, WIDTH), BF16),
            pltpu.VMEM((16, TOK), BF16),
            pltpu.VMEM((GROUP_CHIPS, 2, 16, TOK), BF16),
            pltpu.VMEM((WIDTH, GROUP_CHIPS * 2 * TOK), BF16),
            pltpu.VMEM((2, GROUP_CHIPS * 2 * TOK, WIDTH), F32),
            pltpu.VMEM((2, GROUP_CHIPS, 2, 2, TOK, WIDTH), BF16),
            pltpu.VMEM((2, GROUP_CHIPS, 2, 2, TOK, WIDTH), BF16),
            pltpu.VMEM((2, 2, TOK, SPAN), BF16),
            pltpu.VMEM((KV_HEADS, TOK, SPAN), BF16),
            pltpu.VMEM((2, 2, 2, TOK, WIDTH), F32),
            pltpu.VMEM((2, 16, WIDTH), F32),
            pltpu.VMEM((nz, 8, line), F32),
            pltpu.VMEM((nz, 8, line), F32),
            pltpu.VMEM((8, line), F32),
            pltpu.VMEM((ndp, 8, line), F32),
            pltpu.VMEM((8, line), F32),
            pltpu.VMEM((n, 8, line), F32),
            dma((3,)),
            dma((2, GROUP_CHIPS, 2)), dma((2, GROUP_CHIPS, 2)),
            dma((2, 2)), dma((2, 2)),
            dma((GROUP_CHIPS, 2)), dma((GROUP_CHIPS, 2)),
            dma((2, GROUP_CHIPS, 2)), dma((2, GROUP_CHIPS, 2)),
            dma((2,)), dma((2,)),
            dma((nz,)), dma((nz,)),
            dma((ndp,)), dma((ndp,)),
            dma((n,)), dma((n,)),
        ],
        compiler_params=pltpu.CompilerParams(
            collective_id=0, has_side_effects=True, vmem_limit_bytes=56 * 1024 * 1024
        ),
        name="attention_backward",
    )(*operands)


def position_tables(n):
    half = WIDTH // 2
    inv_freq = 10000.0 ** (-(np.arange(half) * 2.0) / WIDTH)
    angle = inv_freq[None, :, None] * np.arange(n * TOK).reshape(n // 2, 1, 2 * TOK)
    return np.stack([np.cos(angle), np.sin(angle)], axis=1).astype(np.float32)


def local(n, ndp, query, keys, values, out_grad, query_state, value_state, flags):
    tables = jnp.asarray(position_tables(n))
    qg, kg, vg, qa, va = main_call(
        n, ndp, flags, query[0], out_grad[0], keys[0], values[0], query_state[0].T, value_state[0].T, tables
    )
    return qg[None], kg[None], vg[None], qa, va


def solution(mesh):
    split = P("dp", "ctx", None)
    return jax.shard_map(
        functools.partial(local, mesh.shape["ctx"], mesh.shape["dp"]),
        mesh=mesh,
        in_specs=(split,) * 6 + (P(),),
        out_specs=(split, split, split, P(), P()),
        check_vma=False,
    )
```

```python
import functools
import math

import jax
import jax.numpy as jnp
from jax import lax
from jax.experimental import pallas as pl
from jax.experimental.pallas import tpu as pltpu
from jax.sharding import PartitionSpec as P
import numpy as np

KV_HEADS = 4
PER_GROUP = 8
WIDTH = 128
TOK = 128
GROUP_CHIPS = 4
SPAN = PER_GROUP * WIDTH
ADAPTER_SCALE = 2.0
SCORE_SCALE = 1.0 / math.sqrt(WIDTH)
EXP2_SCALE = SCORE_SCALE * math.log2(math.e)
MESH = pl.DeviceIdType.MESH
F32 = jnp.float32
BF16 = jnp.bfloat16


def dot(a, b, dims):
    return lax.dot_general(a, b, (dims, ((), ())), preferred_element_type=F32)


NT = ((1,), (1,))
NN = ((1,), (0,))


STRIP = 64
FOLD = STRIP // 8


def attend(nb, us, first, qb, db, kvb, kT, table, acc, dqb, score, dprob, low_p, low_ds):
    span = nb * 2 * TOK
    n_rows = 4 * TOK
    strips = [slice(i, i + STRIP) for i in range(0, span, STRIP)]
    key = kvb[us, 0:nb, :, 0].reshape(span, WIDTH)
    val = kvb[us, 0:nb, :, 1].reshape(span, WIDTH)
    fold = (FOLD, 8, n_rows)

    def columns(pair, g):
        return pl.ds(pl.multiple_of((first + pair) * 2 * WIDTH + g * WIDTH, WIDTH), WIDTH)

    def rows(ref, pair):
        return jnp.concatenate([ref[us, h, :, columns(pair, g)] for g in range(2) for h in range(2)], axis=0)

    def products(pair):
        score[pair, :span] = dot(key, rows(qb, pair), NT)
        dprob[pair, :span] = dot(val, rows(db, pair), NT)

    def softmax(pair):
        top = jnp.full((8, n_rows), -jnp.inf, F32)
        for at in strips:
            s = score[pair, at]
            if at.start < 2 * TOK:
                kpos = lax.broadcasted_iota(jnp.int32, (STRIP, n_rows), 0) + at.start
                rpos = lax.broadcasted_iota(jnp.int32, (STRIP, n_rows), 1) & (2 * TOK - 1)
                s = jnp.where(kpos <= rpos, s, -jnp.inf)
                score[pair, at] = s
            top = jnp.maximum(top, jnp.max(s.reshape(fold), axis=0))
        top = jnp.max(top, axis=0, keepdims=True)
        total = jnp.zeros((8, n_rows), F32)
        mixed = jnp.zeros((8, n_rows), F32)
        for at in strips:
            weight = jnp.exp2((score[pair, at] - top) * EXP2_SCALE)
            score[pair, at] = weight
            total = total + jnp.sum(weight.reshape(fold), axis=0)
            mixed = mixed + jnp.sum((weight * dprob[pair, at]).reshape(fold), axis=0)
        inverse = 1.0 / jnp.sum(total, axis=0, keepdims=True)
        delta = jnp.sum(mixed, axis=0, keepdims=True) * inverse
        for at in strips:
            prob = score[pair, at] * inverse
            low_p[pair, at] = prob.astype(BF16)
            low_ds[pair, at] = (prob * (dprob[pair, at] - delta)).astype(BF16)

    def gradients(pair):
        acc[1, :span] += dot(low_p[pair, :span], rows(db, pair), NN)
        acc[0, :span] += dot(low_ds[pair, :span], rows(qb, pair), NN)
        dqT = dot(kT[:, :span], low_ds[pair, :span], NN)
        cos = jnp.concatenate([table[0], table[0]], axis=1)
        sin = jnp.concatenate([table[1], table[1]], axis=1)
        front = dqT[: WIDTH // 2] * SCORE_SCALE
        back = dqT[WIDTH // 2 :] * SCORE_SCALE
        turned = jnp.concatenate([front * cos + back * sin, back * cos - front * sin], axis=0)
        dq = turned.T.astype(BF16)
        for g in range(2):
            for h in range(2):
                at = (g * 2 + h) * TOK
                dqb[us, h, :, columns(pair, g)] = dq[at : at + TOK]

    products(0)
    products(1)
    softmax(0)
    gradients(0)
    softmax(1)
    gradients(1)


def main_kernel(
    n, ndp,
    flags, q_hbm, d_hbm, k_in, v_in, sq, sv, tables,
    qgs, kvg, gat,
    q, d, table, qsend, dsend, kv,
    qb, db, kvb, st, stb, kT, acc, psend, rbuf, dqb, own,
    vpart, msg, zr, zsum, dr, res,
    score, dprob, low_p, low_ds,
    loads, kvs, kvr, qs, qr, ss, sr, ps, pr, dqs, dqr,
    zs_s, zr_s, ds_s, dr_s, as_s, ar_s,
):
    nz = n // 2
    wide = 2 * SPAN // nz
    me = lax.axis_index("ctx")
    dpi = lax.axis_index("dp")
    z = me // 2
    c = me % 2
    other = 1 - c
    sib = z * 2 + other

    def slot(us, zz):
        return (zz + 2 * us) % GROUP_CHIPS

    def copy(src, dst, send, recv, target):
        return pltpu.make_async_remote_copy(
            src_ref=src, dst_ref=dst, send_sem=send, recv_sem=recv,
            device_id=target, device_id_type=MESH,
        )

    load_q = pltpu.make_async_copy(q_hbm, q, loads.at[0])
    load_d = pltpu.make_async_copy(d_hbm, d, loads.at[1])
    load_t = pltpu.make_async_copy(tables.at[z], table, loads.at[2])
    load_q.start()
    load_d.start()
    load_t.start()

    barrier = pltpu.get_barrier_semaphore()

    @pl.loop(1, n)
    def _(o):
        pl.semaphore_signal(barrier, inc=1, device_id=(dpi, (me + o) % n), device_id_type=MESH)

    @pl.loop(1, ndp)
    def _(o):
        pl.semaphore_signal(barrier, inc=1, device_id=((dpi + o) % ndp, me), device_id_type=MESH)

    flag = [flags[h] for h in range(KV_HEADS)]

    def same(a, b):
        return 1 - (a - b) * (a - b)

    rank = [sum((same(flag[j], flag[h]) for j in range(h)), jnp.int32(0)) for h in range(KV_HEADS)]

    def share(h, cc, us):
        return (same(rank[h], cc) * same(flag[h], us)).astype(F32)

    def pick(parts, weights):
        total = None
        for part, weight in zip(parts, weights):
            term = part * jnp.full(part.shape, weight, F32).astype(part.dtype)
            total = term if total is None else total + term
        return total

    def gather(ref, width, cc, us):
        heads = range(KV_HEADS)
        return pick([ref[:, h * width : (h + 1) * width] for h in heads], [share(h, cc, us) for h in heads])

    st[...] = jnp.concatenate([sq[...].astype(F32), sv[...].astype(F32)], axis=0).astype(BF16)
    stb[0, c] = st[...]
    for s in range(KV_HEADS):
        kv[s, 0] = gather(k_in, WIDTH, s // 2, s % 2)
        kv[s, 1] = gather(v_in, WIDTH, s // 2, s % 2)
    early = (z // 2) % 2
    load_q.wait()
    load_d.wait()
    for us in range(2):
        qsend[us] = gather(q, SPAN, other, us)
        dsend[us] = gather(d, SPAN, other, us)
        qb[us, c] = gather(q, SPAN, c, us)
        db[us, c] = gather(d, SPAN, c, us)
        kvb[us, 0, c] = kv[2 * c + us]
    load_t.wait()

    pl.semaphore_wait(barrier, n - 1 + ndp - 1)

    def near_kv(us):
        return copy(kv.at[2 * other + us], kvb.at[us, 0, c], kvs.at[us, 0, other], kvr.at[us, 0, c], (dpi, sib))

    def far_kv(us, t, cc):
        zt = (z + t) % nz
        return copy(kv.at[2 * cc + us], kvb.at[us, t, c], kvs.at[us, t, cc], kvr.at[us, t, c], (dpi, 2 * zt + cc))

    def near_rows(us, i):
        src, dst = ((qsend, qb), (dsend, db))[i]
        return copy(src.at[us], dst.at[us, c], qs.at[us, i], qr.at[us, i], (dpi, sib))

    def near_state():
        return copy(st, stb.at[0, c], ss.at[0, other], sr.at[0, c], (dpi, sib))

    def far_state(t, cc):
        zt = (z + t) % nz
        return copy(st, stb.at[t, c], ss.at[t, cc], sr.at[t, c], (dpi, 2 * zt + cc))

    def far_part(us, t, h):
        zo = (z - t + nz) % nz
        return copy(psend.at[us, t, h], rbuf.at[us, t, c], ps.at[us, t, h], pr.at[us, t, c], (dpi, 2 * zo + h))

    def near_part(us):
        return copy(psend.at[us, 0, other], rbuf.at[us, 0, c], ps.at[us, 0, other], pr.at[us, 0, c], (dpi, sib))

    def near_dq(us):
        return copy(dqb.at[us, other], qgs.at[2 * c + us], dqs.at[us], dqr.at[us], (dpi, sib))

    @pl.loop(0, 2)
    def _(step):
        us = (step + early) % 2
        near_kv(us).start()
        near_rows(us, 0).start()
        near_rows(us, 1).start()

        @pl.loop(1, GROUP_CHIPS)
        def _(t):
            @pl.when(t <= slot(us, (z + t) % nz))
            def _():
                far_kv(us, t, 0).start()
                far_kv(us, t, 1).start()

    near_state().start()

    @pl.loop(1, GROUP_CHIPS)
    def _(t):
        far_state(t, 0).start()
        far_state(t, 1).start()

    @pl.loop(0, 2)
    def _(step):
        us = (step + early) % 2
        nb = slot(us, z) + 1
        copy(kv.at[0], kvb.at[us, 0, other], kvs.at[us, 0, other], kvr.at[us, 0, other], (dpi, sib)).wait_recv()
        near_rows(us, 0).wait_recv()
        near_rows(us, 1).wait_recv()

        @pl.loop(1, nb)
        def _(t):
            for h in range(2):
                copy(kv.at[0], kvb.at[us, t, h], kvs.at[us, t, h], kvr.at[us, t, h], (dpi, sib)).wait_recv()

        @pl.loop(0, nb)
        def _(t):
            at = pl.ds(pl.multiple_of(t * 2 * TOK, 2 * TOK), 2 * TOK)
            kT[:, at] = kvb[us, t, :, 0].reshape(2 * TOK, WIDTH).astype(F32).T.astype(BF16)
            acc[0, at] = jnp.zeros((2 * TOK, WIDTH), F32)
            acc[1, at] = jnp.zeros((2 * TOK, WIDTH), F32)

        for count in range(1, GROUP_CHIPS + 1):
            @pl.when(nb == count)
            def _(count=count):
                @pl.loop(0, PER_GROUP // 2, step=2)
                def _(first):
                    attend(count, us, first, qb, db, kvb, kT, table, acc, dqb, score, dprob, low_p, low_ds)

        near_dq(us).start()

        @pl.loop(0, nb)
        def _(t):
            for h in range(2):
                at = pl.ds(pl.multiple_of(t * 2 * TOK + h * TOK, TOK), TOK)
                psend[us, t, h, 0] = acc[0, at].astype(BF16)
                psend[us, t, h, 1] = acc[1, at].astype(BF16)

            @pl.when(t > 0)
            def _():
                far_part(us, t, 0).start()
                far_part(us, t, 1).start()

        near_part(us).start()

        @pl.when(step == 0)
        def _():
            copy(st, stb.at[0, other], ss.at[0, other], sr.at[0, other], (dpi, sib)).wait_recv()

            @pl.loop(1, GROUP_CHIPS)
            def _(t):
                for h in range(2):
                    copy(st, stb.at[t, h], ss.at[t, h], sr.at[t, h], (dpi, sib)).wait_recv()

        part = dot(stb[0, 0], dqb[us, 0], NN) + dot(stb[0, 1], dqb[us, 1], NN)
        for j in range(nz // 2):
            msg[us * (nz // 2) + j, :, :wide] = part[:8, j * wide : (j + 1) * wide]

        def value_term(t, x):
            return x + dot(stb[t, 0], psend[us, t, 0, 1], NN) + dot(stb[t, 1], psend[us, t, 1, 1], NN)

        vpart[us] = lax.fori_loop(0, nb, value_term, jnp.zeros((16, WIDTH), F32))
        rbuf[us, 0, c] = psend[us, 0, c]
        qgs[2 * c + us] = dqb[us, c]

    for k in range(nz):
        for us in range(2):
            msg[k, :, wide + us * WIDTH : wide + (us + 1) * WIDTH] = vpart[us, 8:]

    def to_chip(k):
        return copy(msg.at[k], zr.at[z], zs_s.at[k], zr_s.at[z], (dpi, 2 * k + c))

    @pl.loop(1, nz)
    def _(o):
        to_chip((z + o) % nz).start()

    zr[z] = msg[z]

    @pl.loop(1, nz)
    def _(o):
        k = (z + o) % nz
        copy(msg.at[k], zr.at[k], zs_s.at[k], zr_s.at[k], (dpi, sib)).wait_recv()

    zsum[...] = lax.fori_loop(0, nz, lambda k, x: x + zr[k], jnp.zeros((8, wide + 2 * WIDTH), F32))

    def to_dp(o):
        return copy(zsum, dr.at[dpi], ds_s.at[o], dr_s.at[dpi], ((dpi + o) % ndp, me))

    @pl.loop(1, ndp)
    def _(o):
        to_dp(o).start()

    dr[dpi] = zsum[...]

    def owner_sum(us):
        copy(kv.at[0], rbuf.at[us, 0, other], ps.at[us, 0, other], pr.at[us, 0, other], (dpi, sib)).wait_recv()
        for cc in range(2):
            own[us, cc] = rbuf[us, 0, cc].astype(F32)

        @pl.loop(1, GROUP_CHIPS)
        def _(t):
            @pl.when(t <= slot(us, (z + t) % nz))
            def _():
                for cc in range(2):
                    copy(kv.at[0], rbuf.at[us, t, cc], ps.at[us, t, cc], pr.at[us, t, cc], (dpi, sib)).wait_recv()
                    own[us, cc] += rbuf[us, t, cc].astype(F32)

    @pl.loop(1, ndp)
    def _(o):
        k = (dpi + o) % ndp
        copy(zsum, dr.at[k], ds_s.at[o], dr_s.at[k], (dpi, sib)).wait_recv()

    res[...] = (
        lax.fori_loop(0, ndp, lambda k, x: x + dr[k], jnp.zeros((8, wide + 2 * WIDTH), F32)) * ADAPTER_SCALE
    )

    def to_ctx(o):
        return copy(res, gat.at[me], as_s.at[o], ar_s.at[me], (dpi, (me + o) % n))

    @pl.loop(1, n)
    def _(o):
        to_ctx(o).start()

    gat[me] = res[...]

    @pl.loop(0, 2)
    def _(us):
        copy(dqb.at[us, other], qgs.at[2 * other + us], dqs.at[us], dqr.at[us], (dpi, sib)).wait_recv()

    @pl.loop(0, 2)
    def _(us):
        owner_sum(us)

    cos = jnp.where(c == 0, table[0, :, :TOK], table[0, :, TOK:]).T
    sin = jnp.where(c == 0, table[1, :, :TOK], table[1, :, TOK:]).T
    cos = jnp.concatenate([cos, cos], axis=1)
    sin = jnp.concatenate([sin, -sin], axis=1)
    for cc in range(2):
        for us in range(2):
            dk = own[us, cc, 0] * SCORE_SCALE
            kvg[2 * cc + us, 0] = (dk * cos + pltpu.roll(dk, WIDTH // 2, 1) * sin).astype(BF16)
            kvg[2 * cc + us, 1] = own[us, cc, 1].astype(BF16)

    @pl.loop(1, n)
    def _(o):
        k = (me + o) % n
        copy(res, gat.at[k], as_s.at[o], ar_s.at[k], (dpi, sib)).wait_recv()

    @pl.loop(0, 2)
    def _(us):
        near_dq(us).wait_send()
        near_kv(us).wait_send()
        near_rows(us, 0).wait_send()
        near_rows(us, 1).wait_send()
        near_part(us).wait_send()

        @pl.loop(1, GROUP_CHIPS)
        def _(t):
            @pl.when(t <= slot(us, (z + t) % nz))
            def _():
                far_kv(us, t, 0).wait_send()
                far_kv(us, t, 1).wait_send()

            @pl.when(t <= slot(us, z))
            def _():
                far_part(us, t, 0).wait_send()
                far_part(us, t, 1).wait_send()

    near_state().wait_send()

    @pl.loop(1, GROUP_CHIPS)
    def _(t):
        far_state(t, 0).wait_send()
        far_state(t, 1).wait_send()

    @pl.loop(1, nz)
    def _(o):
        to_chip((z + o) % nz).wait_send()

    @pl.loop(1, ndp)
    def _(o):
        to_dp(o).wait_send()

    @pl.loop(1, n)
    def _(o):
        to_ctx(o).wait_send()


def main_call(n, ndp, *operands):
    nz = n // 2
    line = 2 * SPAN // nz + 2 * WIDTH
    vmem = pl.BlockSpec(memory_space=pltpu.VMEM)
    smem = pl.BlockSpec(memory_space=pltpu.SMEM)
    away = pl.BlockSpec(memory_space=pl.ANY)
    dma = pltpu.SemaphoreType.DMA
    return pl.pallas_call(
        functools.partial(main_kernel, n, ndp),
        in_specs=[smem, away, away, vmem, vmem, vmem, vmem, away],
        out_specs=[vmem] * 3,
        out_shape=[
            jax.ShapeDtypeStruct((KV_HEADS, TOK, SPAN), BF16),
            jax.ShapeDtypeStruct((KV_HEADS, 2, TOK, WIDTH), BF16),
            jax.ShapeDtypeStruct((n, 8, line), F32),
        ],
        scratch_shapes=[
            pltpu.VMEM((TOK, KV_HEADS * SPAN), BF16),
            pltpu.VMEM((TOK, KV_HEADS * SPAN), BF16),
            pltpu.VMEM((2, WIDTH // 2, 2 * TOK), F32),
            pltpu.VMEM((2, TOK, SPAN), BF16),
            pltpu.VMEM((2, TOK, SPAN), BF16),
            pltpu.VMEM((KV_HEADS, 2, TOK, WIDTH), BF16),
            pltpu.VMEM((2, 2, TOK, SPAN), BF16),
            pltpu.VMEM((2, 2, TOK, SPAN), BF16),
            pltpu.VMEM((2, GROUP_CHIPS, 2, 2, TOK, WIDTH), BF16),
            pltpu.VMEM((16, TOK), BF16),
            pltpu.VMEM((GROUP_CHIPS, 2, 16, TOK), BF16),
            pltpu.VMEM((WIDTH, GROUP_CHIPS * 2 * TOK), BF16),
            pltpu.VMEM((2, GROUP_CHIPS * 2 * TOK, WIDTH), F32),
            pltpu.VMEM((2, GROUP_CHIPS, 2, 2, TOK, WIDTH), BF16),
            pltpu.VMEM((2, GROUP_CHIPS, 2, 2, TOK, WIDTH), BF16),
            pltpu.VMEM((2, 2, TOK, SPAN), BF16),
            pltpu.VMEM((2, 2, 2, TOK, WIDTH), F32),
            pltpu.VMEM((2, 16, WIDTH), F32),
            pltpu.VMEM((nz, 8, line), F32),
            pltpu.VMEM((nz, 8, line), F32),
            pltpu.VMEM((8, line), F32),
            pltpu.VMEM((ndp, 8, line), F32),
            pltpu.VMEM((8, line), F32),
            pltpu.VMEM((2, GROUP_CHIPS * 2 * TOK, 4 * TOK), F32),
            pltpu.VMEM((2, GROUP_CHIPS * 2 * TOK, 4 * TOK), F32),
            pltpu.VMEM((2, GROUP_CHIPS * 2 * TOK, 4 * TOK), BF16),
            pltpu.VMEM((2, GROUP_CHIPS * 2 * TOK, 4 * TOK), BF16),
            dma((3,)),
            dma((2, GROUP_CHIPS, 2)), dma((2, GROUP_CHIPS, 2)),
            dma((2, 2)), dma((2, 2)),
            dma((GROUP_CHIPS, 2)), dma((GROUP_CHIPS, 2)),
            dma((2, GROUP_CHIPS, 2)), dma((2, GROUP_CHIPS, 2)),
            dma((2,)), dma((2,)),
            dma((nz,)), dma((nz,)),
            dma((ndp,)), dma((ndp,)),
            dma((n,)), dma((n,)),
        ],
        compiler_params=pltpu.CompilerParams(
            collective_id=0, has_side_effects=True, vmem_limit_bytes=48 * 1024 * 1024
        ),
        name="attention_backward",
    )(*operands)


def restore_kernel(n, flags, qgs, kvg, gat, qg, kg, vg, qa, va):
    nz = n // 2
    wide = 2 * SPAN // nz
    for h in range(KV_HEADS):
        us = flags[h]
        cc = sum((jnp.where(flags[j] == us, 1, 0) for j in range(h)), jnp.int32(0))
        qg[:, h * SPAN : (h + 1) * SPAN] = qgs[2 * cc + us]
        kg[:, h * WIDTH : (h + 1) * WIDTH] = kvg[2 * cc + us, 0]
        vg[:, h * WIDTH : (h + 1) * WIDTH] = kvg[2 * cc + us, 1]
        for j in range(nz // 2):
            at = h * SPAN + j * wide
            qa[:, at : at + wide] = gat[2 * (us * (nz // 2) + j) + cc, :, :wide]
        at = pl.ds(pl.multiple_of(wide + us * WIDTH, WIDTH), WIDTH)
        va[:, h * WIDTH : (h + 1) * WIDTH] = gat[cc, :, at]


def restore(n, flags, *operands):
    vmem = pl.BlockSpec(memory_space=pltpu.VMEM)
    hw = KV_HEADS * WIDTH
    return pl.pallas_call(
        functools.partial(restore_kernel, n),
        in_specs=[pl.BlockSpec(memory_space=pltpu.SMEM)] + [vmem] * 3,
        out_specs=[vmem] * 5,
        out_shape=[
            jax.ShapeDtypeStruct((TOK, KV_HEADS * SPAN), BF16),
            jax.ShapeDtypeStruct((TOK, hw), BF16),
            jax.ShapeDtypeStruct((TOK, hw), BF16),
            jax.ShapeDtypeStruct((8, KV_HEADS * SPAN), F32),
            jax.ShapeDtypeStruct((8, hw), F32),
        ],
        compiler_params=pltpu.CompilerParams(vmem_limit_bytes=16 * 1024 * 1024),
        name="restore_heads",
    )(flags, *operands)


def position_tables(n):
    half = WIDTH // 2
    inv_freq = 10000.0 ** (-(np.arange(half) * 2.0) / WIDTH)
    angle = inv_freq[None, :, None] * np.arange(n * TOK).reshape(n // 2, 1, 2 * TOK)
    return np.stack([np.cos(angle), np.sin(angle)], axis=1).astype(np.float32)


def local(n, ndp, query, keys, values, out_grad, query_state, value_state, flags):
    tables = jnp.asarray(position_tables(n))
    places = main_call(
        n, ndp, flags, query[0], out_grad[0], keys[0], values[0], query_state[0].T, value_state[0].T, tables
    )
    qg, kg, vg, qa, va = restore(n, flags, *places)
    return qg[None], kg[None], vg[None], qa, va


def solution(mesh):
    split = P("dp", "ctx", None)
    return jax.shard_map(
        functools.partial(local, mesh.shape["ctx"], mesh.shape["dp"]),
        mesh=mesh,
        in_specs=(split,) * 6 + (P(),),
        out_specs=(split, split, split, P(), P()),
        check_vma=False,
    )
```

```python
import functools
import math

import jax
import jax.numpy as jnp
from jax import lax
from jax.experimental import pallas as pl
from jax.experimental.pallas import tpu as pltpu
from jax.sharding import PartitionSpec as P
import numpy as np

KV_HEADS = 4
PER_GROUP = 8
WIDTH = 128
TOK = 128
GROUP_CHIPS = 4
SPAN = PER_GROUP * WIDTH
ADAPTER_SCALE = 2.0
SCORE_SCALE = 1.0 / math.sqrt(WIDTH)
EXP2_SCALE = SCORE_SCALE * math.log2(math.e)
MESH = pl.DeviceIdType.MESH
F32 = jnp.float32
BF16 = jnp.bfloat16


def dot(a, b, dims):
    return lax.dot_general(a, b, (dims, ((), ())), preferred_element_type=F32)


NT = ((1,), (1,))
NN = ((1,), (0,))


STRIP = 64
BLOCK = 2 * TOK
PAIRS = PER_GROUP // 2
ROWS = 4 * TOK


def fold(x):
    return x.reshape(x.shape[0] // 8, 8, x.shape[1])


def spread(x):
    return jnp.broadcast_to(x, (8, x.shape[1]))


def main_kernel(
    n, ndp,
    flags, q_hbm, d_hbm, k_in, v_in, sq, sv, tables,
    qgs, kvg, gat,
    q, d, table, qsend, dsend, kv,
    qb, db, kvb, st, stb, kT, psend, rbuf, dqb, own,
    vpart, msg, zr, zsum, dr, res,
    score, dprob, low_p, low_ds, dqT, top, total, mixed,
    loads, kvs, kvr, qs, qr, ss, sr, ps, pr, dqs, dqr,
    zs_s, zr_s, ds_s, dr_s, as_s, ar_s,
):
    nz = n // 2
    wide = 2 * SPAN // nz
    me = lax.axis_index("ctx")
    dpi = lax.axis_index("dp")
    z = me // 2
    c = me % 2
    other = 1 - c
    sib = z * 2 + other

    def slot(us, zz):
        return (zz + 2 * us) % GROUP_CHIPS

    def copy(src, dst, send, recv, target):
        return pltpu.make_async_remote_copy(
            src_ref=src, dst_ref=dst, send_sem=send, recv_sem=recv,
            device_id=target, device_id_type=MESH,
        )

    load_q = pltpu.make_async_copy(q_hbm, q, loads.at[0])
    load_d = pltpu.make_async_copy(d_hbm, d, loads.at[1])
    load_t = pltpu.make_async_copy(tables.at[z], table, loads.at[2])
    load_q.start()
    load_d.start()
    load_t.start()

    barrier = pltpu.get_barrier_semaphore()

    @pl.loop(1, n)
    def _(o):
        pl.semaphore_signal(barrier, inc=1, device_id=(dpi, (me + o) % n), device_id_type=MESH)

    @pl.loop(1, ndp)
    def _(o):
        pl.semaphore_signal(barrier, inc=1, device_id=((dpi + o) % ndp, me), device_id_type=MESH)

    flag = [flags[h] for h in range(KV_HEADS)]

    def same(a, b):
        return 1 - (a - b) * (a - b)

    rank = [sum((same(flag[j], flag[h]) for j in range(h)), jnp.int32(0)) for h in range(KV_HEADS)]

    def share(h, cc, us):
        return (same(rank[h], cc) * same(flag[h], us)).astype(F32)

    def pick(parts, weights):
        total = None
        for part, weight in zip(parts, weights):
            term = part * jnp.full(part.shape, weight, F32).astype(part.dtype)
            total = term if total is None else total + term
        return total

    def gather(ref, width, cc, us):
        heads = range(KV_HEADS)
        return pick([ref[:, h * width : (h + 1) * width] for h in heads], [share(h, cc, us) for h in heads])

    st[...] = jnp.concatenate([sq[...].astype(F32), sv[...].astype(F32)], axis=0).astype(BF16)
    stb[0, c] = st[...]
    for s in range(KV_HEADS):
        kv[s, 0] = gather(k_in, WIDTH, s // 2, s % 2)
        kv[s, 1] = gather(v_in, WIDTH, s // 2, s % 2)
    early = (z // 2) % 2
    load_q.wait()
    load_d.wait()
    for us in range(2):
        qsend[us] = gather(q, SPAN, other, us)
        dsend[us] = gather(d, SPAN, other, us)
        qb[us, c] = gather(q, SPAN, c, us)
        db[us, c] = gather(d, SPAN, c, us)
        kvb[us, 0, c] = kv[2 * c + us]
    load_t.wait()

    pl.semaphore_wait(barrier, n - 1 + ndp - 1)

    def near_kv(us):
        return copy(kv.at[2 * other + us], kvb.at[us, 0, c], kvs.at[us, 0, other], kvr.at[us, 0, c], (dpi, sib))

    def far_kv(us, t, cc):
        zt = (z + t) % nz
        return copy(kv.at[2 * cc + us], kvb.at[us, t, c], kvs.at[us, t, cc], kvr.at[us, t, c], (dpi, 2 * zt + cc))

    def near_rows(us, i):
        src, dst = ((qsend, qb), (dsend, db))[i]
        return copy(src.at[us], dst.at[us, c], qs.at[us, i], qr.at[us, i], (dpi, sib))

    def near_state():
        return copy(st, stb.at[0, c], ss.at[0, other], sr.at[0, c], (dpi, sib))

    def far_state(t, cc):
        zt = (z + t) % nz
        return copy(st, stb.at[t, c], ss.at[t, cc], sr.at[t, c], (dpi, 2 * zt + cc))

    def far_part(us, t, h):
        zo = (z - t + nz) % nz
        return copy(psend.at[us, t, h], rbuf.at[us, t, c], ps.at[us, t, h], pr.at[us, t, c], (dpi, 2 * zo + h))

    def near_part(us):
        return copy(psend.at[us, 0, other], rbuf.at[us, 0, c], ps.at[us, 0, other], pr.at[us, 0, c], (dpi, sib))

    def near_dq(us):
        return copy(dqb.at[us, other], qgs.at[2 * c + us], dqs.at[us], dqr.at[us], (dpi, sib))

    @pl.loop(0, 2)
    def _(step):
        us = (step + early) % 2
        near_kv(us).start()
        near_rows(us, 0).start()
        near_rows(us, 1).start()

        @pl.loop(1, GROUP_CHIPS)
        def _(t):
            @pl.when(t <= slot(us, (z + t) % nz))
            def _():
                far_kv(us, t, 0).start()
                far_kv(us, t, 1).start()

    near_state().start()

    @pl.loop(1, GROUP_CHIPS)
    def _(t):
        far_state(t, 0).start()
        far_state(t, 1).start()

    @pl.loop(0, 2)
    def _(step):
        us = (step + early) % 2
        nb = slot(us, z) + 1
        copy(kv.at[0], kvb.at[us, 0, other], kvs.at[us, 0, other], kvr.at[us, 0, other], (dpi, sib)).wait_recv()
        near_rows(us, 0).wait_recv()
        near_rows(us, 1).wait_recv()
        for pair in range(PAIRS):
            top[pair] = jnp.full((8, ROWS), -jnp.inf, F32)
            total[pair] = jnp.zeros((8, ROWS), F32)
            mixed[pair] = jnp.zeros((8, ROWS), F32)

        def rows(ref, pair):
            heads = [slice((2 * pair + g) * WIDTH, (2 * pair + g + 1) * WIDTH) for g in range(2)]
            return jnp.concatenate([ref[us, h, :, heads[g]] for g in range(2) for h in range(2)], axis=0)

        @pl.loop(0, nb)
        def _(t):
            @pl.when(t > 0)
            def _():
                for h in range(2):
                    copy(kv.at[0], kvb.at[us, t, h], kvs.at[us, t, h], kvr.at[us, t, h], (dpi, sib)).wait_recv()

            key = kvb[us, t, :, 0].reshape(BLOCK, WIDTH)
            val = kvb[us, t, :, 1].reshape(BLOCK, WIDTH)
            at = pl.ds(pl.multiple_of(t * BLOCK, BLOCK), BLOCK)
            kT[:, at] = key.astype(F32).T.astype(BF16)
            kpos = lax.broadcasted_iota(jnp.int32, (BLOCK, ROWS), 0)
            rpos = lax.broadcasted_iota(jnp.int32, (BLOCK, ROWS), 1) & (BLOCK - 1)
            seen = kpos <= rpos + t * BLOCK
            for pair in range(PAIRS):
                s = jnp.where(seen, dot(key, rows(qb, pair), NT), -jnp.inf)
                score[pair, t] = s
                top[pair] = jnp.maximum(top[pair], jnp.max(fold(s), axis=0))
                dprob[pair, t] = dot(val, rows(db, pair), NT)

        for pair in range(PAIRS):
            top[pair] = spread(jnp.max(top[pair], axis=0, keepdims=True))

        @pl.loop(0, nb)
        def _(t):
            for pair in range(PAIRS):
                high = top[pair]
                sum_w = total[pair]
                sum_m = mixed[pair]
                for i in range(0, BLOCK, STRIP):
                    at = slice(i, i + STRIP)
                    weight = jnp.exp2((fold(score[pair, t, at]) - high) * EXP2_SCALE)
                    score[pair, t, at] = weight.reshape(STRIP, ROWS)
                    sum_w = sum_w + jnp.sum(weight, axis=0)
                    sum_m = sum_m + jnp.sum(weight * fold(dprob[pair, t, at]), axis=0)
                total[pair] = sum_w
                mixed[pair] = sum_m

        for pair in range(PAIRS):
            inverse = 1.0 / jnp.sum(total[pair], axis=0, keepdims=True)
            delta = jnp.sum(mixed[pair], axis=0, keepdims=True) * inverse
            total[pair] = spread(inverse)
            mixed[pair] = spread(delta)

        @pl.loop(0, nb)
        def _(back):
            t = nb - 1 - back
            dk = jnp.zeros((BLOCK, WIDTH), F32)
            dv = jnp.zeros((BLOCK, WIDTH), F32)
            for pair in range(PAIRS):
                inverse = total[pair]
                delta = mixed[pair]
                for i in range(0, BLOCK, STRIP):
                    at = slice(i, i + STRIP)
                    prob = fold(score[pair, t, at]) * inverse
                    ds = prob * (fold(dprob[pair, t, at]) - delta)
                    low_p[pair, at] = prob.reshape(STRIP, ROWS).astype(BF16)
                    low_ds[pair, t, at] = ds.reshape(STRIP, ROWS).astype(BF16)
                dv = dv + dot(low_p[pair], rows(db, pair), NN)
                dk = dk + dot(low_ds[pair, t], rows(qb, pair), NN)
            for h in range(2):
                psend[us, t, h, 0] = dk[h * TOK : (h + 1) * TOK].astype(BF16)
                psend[us, t, h, 1] = dv[h * TOK : (h + 1) * TOK].astype(BF16)

            @pl.when(t > 0)
            def _():
                far_part(us, t, 0).start()
                far_part(us, t, 1).start()

        near_part(us).start()

        for count in range(1, GROUP_CHIPS + 1):
            @pl.when(nb == count)
            def _(count=count):
                for pair in range(PAIRS):
                    ds = low_ds[pair, 0:count].reshape(count * BLOCK, ROWS)
                    dqT[pair] = dot(kT[:, : count * BLOCK], ds, NN)

        cos = jnp.concatenate([table[0], table[0]], axis=1)
        sin = jnp.concatenate([table[1], table[1]], axis=1)
        for pair in range(PAIRS):
            front = dqT[pair, : WIDTH // 2] * SCORE_SCALE
            back = dqT[pair, WIDTH // 2 :] * SCORE_SCALE
            turned = jnp.concatenate([front * cos + back * sin, back * cos - front * sin], axis=0)
            dq = turned.T.astype(BF16)
            for g in range(2):
                for h in range(2):
                    at = (g * 2 + h) * TOK
                    dqb[us, h, :, (2 * pair + g) * WIDTH : (2 * pair + g + 1) * WIDTH] = dq[at : at + TOK]
        near_dq(us).start()

        @pl.when(step == 0)
        def _():
            copy(st, stb.at[0, other], ss.at[0, other], sr.at[0, other], (dpi, sib)).wait_recv()

            @pl.loop(1, GROUP_CHIPS)
            def _(t):
                for h in range(2):
                    copy(st, stb.at[t, h], ss.at[t, h], sr.at[t, h], (dpi, sib)).wait_recv()

        part = dot(stb[0, 0], dqb[us, 0], NN) + dot(stb[0, 1], dqb[us, 1], NN)
        for j in range(nz // 2):
            msg[us * (nz // 2) + j, :, :wide] = part[:8, j * wide : (j + 1) * wide]

        def value_term(t, x):
            return x + dot(stb[t, 0], psend[us, t, 0, 1], NN) + dot(stb[t, 1], psend[us, t, 1, 1], NN)

        vpart[us] = lax.fori_loop(0, nb, value_term, jnp.zeros((16, WIDTH), F32))
        rbuf[us, 0, c] = psend[us, 0, c]
        qgs[2 * c + us] = dqb[us, c]

    for k in range(nz):
        for us in range(2):
            msg[k, :, wide + us * WIDTH : wide + (us + 1) * WIDTH] = vpart[us, 8:]

    def to_chip(k):
        return copy(msg.at[k], zr.at[z], zs_s.at[k], zr_s.at[z], (dpi, 2 * k + c))

    @pl.loop(1, nz)
    def _(o):
        to_chip((z + o) % nz).start()

    zr[z] = msg[z]

    @pl.loop(1, nz)
    def _(o):
        k = (z + o) % nz
        copy(msg.at[k], zr.at[k], zs_s.at[k], zr_s.at[k], (dpi, sib)).wait_recv()

    zsum[...] = lax.fori_loop(0, nz, lambda k, x: x + zr[k], jnp.zeros((8, wide + 2 * WIDTH), F32))

    def to_dp(o):
        return copy(zsum, dr.at[dpi], ds_s.at[o], dr_s.at[dpi], ((dpi + o) % ndp, me))

    @pl.loop(1, ndp)
    def _(o):
        to_dp(o).start()

    dr[dpi] = zsum[...]

    def owner_sum(us):
        copy(kv.at[0], rbuf.at[us, 0, other], ps.at[us, 0, other], pr.at[us, 0, other], (dpi, sib)).wait_recv()
        for cc in range(2):
            own[us, cc] = rbuf[us, 0, cc].astype(F32)

        @pl.loop(1, GROUP_CHIPS)
        def _(t):
            @pl.when(t <= slot(us, (z + t) % nz))
            def _():
                for cc in range(2):
                    copy(kv.at[0], rbuf.at[us, t, cc], ps.at[us, t, cc], pr.at[us, t, cc], (dpi, sib)).wait_recv()
                    own[us, cc] += rbuf[us, t, cc].astype(F32)

    @pl.loop(1, ndp)
    def _(o):
        k = (dpi + o) % ndp
        copy(zsum, dr.at[k], ds_s.at[o], dr_s.at[k], (dpi, sib)).wait_recv()

    res[...] = (
        lax.fori_loop(0, ndp, lambda k, x: x + dr[k], jnp.zeros((8, wide + 2 * WIDTH), F32)) * ADAPTER_SCALE
    )

    def to_ctx(o):
        return copy(res, gat.at[me], as_s.at[o], ar_s.at[me], (dpi, (me + o) % n))

    @pl.loop(1, n)
    def _(o):
        to_ctx(o).start()

    gat[me] = res[...]

    @pl.loop(0, 2)
    def _(us):
        copy(dqb.at[us, other], qgs.at[2 * other + us], dqs.at[us], dqr.at[us], (dpi, sib)).wait_recv()

    @pl.loop(0, 2)
    def _(us):
        owner_sum(us)

    cos = jnp.where(c == 0, table[0, :, :TOK], table[0, :, TOK:]).T
    sin = jnp.where(c == 0, table[1, :, :TOK], table[1, :, TOK:]).T
    cos = jnp.concatenate([cos, cos], axis=1)
    sin = jnp.concatenate([sin, -sin], axis=1)
    for cc in range(2):
        for us in range(2):
            dk = own[us, cc, 0] * SCORE_SCALE
            kvg[2 * cc + us, 0] = (dk * cos + pltpu.roll(dk, WIDTH // 2, 1) * sin).astype(BF16)
            kvg[2 * cc + us, 1] = own[us, cc, 1].astype(BF16)

    @pl.loop(1, n)
    def _(o):
        k = (me + o) % n
        copy(res, gat.at[k], as_s.at[o], ar_s.at[k], (dpi, sib)).wait_recv()

    @pl.loop(0, 2)
    def _(us):
        near_dq(us).wait_send()
        near_kv(us).wait_send()
        near_rows(us, 0).wait_send()
        near_rows(us, 1).wait_send()
        near_part(us).wait_send()

        @pl.loop(1, GROUP_CHIPS)
        def _(t):
            @pl.when(t <= slot(us, (z + t) % nz))
            def _():
                far_kv(us, t, 0).wait_send()
                far_kv(us, t, 1).wait_send()

            @pl.when(t <= slot(us, z))
            def _():
                far_part(us, t, 0).wait_send()
                far_part(us, t, 1).wait_send()

    near_state().wait_send()

    @pl.loop(1, GROUP_CHIPS)
    def _(t):
        far_state(t, 0).wait_send()
        far_state(t, 1).wait_send()

    @pl.loop(1, nz)
    def _(o):
        to_chip((z + o) % nz).wait_send()

    @pl.loop(1, ndp)
    def _(o):
        to_dp(o).wait_send()

    @pl.loop(1, n)
    def _(o):
        to_ctx(o).wait_send()


def main_call(n, ndp, *operands):
    nz = n // 2
    line = 2 * SPAN // nz + 2 * WIDTH
    vmem = pl.BlockSpec(memory_space=pltpu.VMEM)
    smem = pl.BlockSpec(memory_space=pltpu.SMEM)
    away = pl.BlockSpec(memory_space=pl.ANY)
    dma = pltpu.SemaphoreType.DMA
    return pl.pallas_call(
        functools.partial(main_kernel, n, ndp),
        in_specs=[smem, away, away, vmem, vmem, vmem, vmem, away],
        out_specs=[vmem] * 3,
        out_shape=[
            jax.ShapeDtypeStruct((KV_HEADS, TOK, SPAN), BF16),
            jax.ShapeDtypeStruct((KV_HEADS, 2, TOK, WIDTH), BF16),
            jax.ShapeDtypeStruct((n, 8, line), F32),
        ],
        scratch_shapes=[
            pltpu.VMEM((TOK, KV_HEADS * SPAN), BF16),
            pltpu.VMEM((TOK, KV_HEADS * SPAN), BF16),
            pltpu.VMEM((2, WIDTH // 2, 2 * TOK), F32),
            pltpu.VMEM((2, TOK, SPAN), BF16),
            pltpu.VMEM((2, TOK, SPAN), BF16),
            pltpu.VMEM((KV_HEADS, 2, TOK, WIDTH), BF16),
            pltpu.VMEM((2, 2, TOK, SPAN), BF16),
            pltpu.VMEM((2, 2, TOK, SPAN), BF16),
            pltpu.VMEM((2, GROUP_CHIPS, 2, 2, TOK, WIDTH), BF16),
            pltpu.VMEM((16, TOK), BF16),
            pltpu.VMEM((GROUP_CHIPS, 2, 16, TOK), BF16),
            pltpu.VMEM((WIDTH, GROUP_CHIPS * 2 * TOK), BF16),
            pltpu.VMEM((2, GROUP_CHIPS, 2, 2, TOK, WIDTH), BF16),
            pltpu.VMEM((2, GROUP_CHIPS, 2, 2, TOK, WIDTH), BF16),
            pltpu.VMEM((2, 2, TOK, SPAN), BF16),
            pltpu.VMEM((2, 2, 2, TOK, WIDTH), F32),
            pltpu.VMEM((2, 16, WIDTH), F32),
            pltpu.VMEM((nz, 8, line), F32),
            pltpu.VMEM((nz, 8, line), F32),
            pltpu.VMEM((8, line), F32),
            pltpu.VMEM((ndp, 8, line), F32),
            pltpu.VMEM((8, line), F32),
            pltpu.VMEM((PAIRS, GROUP_CHIPS, BLOCK, ROWS), F32),
            pltpu.VMEM((PAIRS, GROUP_CHIPS, BLOCK, ROWS), F32),
            pltpu.VMEM((PAIRS, BLOCK, ROWS), BF16),
            pltpu.VMEM((PAIRS, GROUP_CHIPS, BLOCK, ROWS), BF16),
            pltpu.VMEM((PAIRS, WIDTH, ROWS), F32),
            pltpu.VMEM((PAIRS, 8, ROWS), F32),
            pltpu.VMEM((PAIRS, 8, ROWS), F32),
            pltpu.VMEM((PAIRS, 8, ROWS), F32),
            dma((3,)),
            dma((2, GROUP_CHIPS, 2)), dma((2, GROUP_CHIPS, 2)),
            dma((2, 2)), dma((2, 2)),
            dma((GROUP_CHIPS, 2)), dma((GROUP_CHIPS, 2)),
            dma((2, GROUP_CHIPS, 2)), dma((2, GROUP_CHIPS, 2)),
            dma((2,)), dma((2,)),
            dma((nz,)), dma((nz,)),
            dma((ndp,)), dma((ndp,)),
            dma((n,)), dma((n,)),
        ],
        compiler_params=pltpu.CompilerParams(
            collective_id=0, has_side_effects=True, vmem_limit_bytes=56 * 1024 * 1024
        ),
        name="attention_backward",
    )(*operands)


def restore_kernel(n, flags, qgs, kvg, gat, qg, kg, vg, qa, va):
    nz = n // 2
    wide = 2 * SPAN // nz
    for h in range(KV_HEADS):
        us = flags[h]
        cc = sum((jnp.where(flags[j] == us, 1, 0) for j in range(h)), jnp.int32(0))
        qg[:, h * SPAN : (h + 1) * SPAN] = qgs[2 * cc + us]
        kg[:, h * WIDTH : (h + 1) * WIDTH] = kvg[2 * cc + us, 0]
        vg[:, h * WIDTH : (h + 1) * WIDTH] = kvg[2 * cc + us, 1]
        for j in range(nz // 2):
            at = h * SPAN + j * wide
            qa[:, at : at + wide] = gat[2 * (us * (nz // 2) + j) + cc, :, :wide]
        at = pl.ds(pl.multiple_of(wide + us * WIDTH, WIDTH), WIDTH)
        va[:, h * WIDTH : (h + 1) * WIDTH] = gat[cc, :, at]


def restore(n, flags, *operands):
    vmem = pl.BlockSpec(memory_space=pltpu.VMEM)
    hw = KV_HEADS * WIDTH
    return pl.pallas_call(
        functools.partial(restore_kernel, n),
        in_specs=[pl.BlockSpec(memory_space=pltpu.SMEM)] + [vmem] * 3,
        out_specs=[vmem] * 5,
        out_shape=[
            jax.ShapeDtypeStruct((TOK, KV_HEADS * SPAN), BF16),
            jax.ShapeDtypeStruct((TOK, hw), BF16),
            jax.ShapeDtypeStruct((TOK, hw), BF16),
            jax.ShapeDtypeStruct((8, KV_HEADS * SPAN), F32),
            jax.ShapeDtypeStruct((8, hw), F32),
        ],
        compiler_params=pltpu.CompilerParams(vmem_limit_bytes=16 * 1024 * 1024),
        name="restore_heads",
    )(flags, *operands)


def position_tables(n):
    half = WIDTH // 2
    inv_freq = 10000.0 ** (-(np.arange(half) * 2.0) / WIDTH)
    angle = inv_freq[None, :, None] * np.arange(n * TOK).reshape(n // 2, 1, 2 * TOK)
    return np.stack([np.cos(angle), np.sin(angle)], axis=1).astype(np.float32)


def local(n, ndp, query, keys, values, out_grad, query_state, value_state, flags):
    tables = jnp.asarray(position_tables(n))
    places = main_call(
        n, ndp, flags, query[0], out_grad[0], keys[0], values[0], query_state[0].T, value_state[0].T, tables
    )
    qg, kg, vg, qa, va = restore(n, flags, *places)
    return qg[None], kg[None], vg[None], qa, va


def solution(mesh):
    split = P("dp", "ctx", None)
    return jax.shard_map(
        functools.partial(local, mesh.shape["ctx"], mesh.shape["dp"]),
        mesh=mesh,
        in_specs=(split,) * 6 + (P(),),
        out_specs=(split, split, split, P(), P()),
        check_vma=False,
    )
```

```python
import functools
import math

import jax
import jax.numpy as jnp
from jax import lax
from jax.experimental import pallas as pl
from jax.experimental.pallas import tpu as pltpu
from jax.sharding import PartitionSpec as P
import numpy as np

KV_HEADS = 4
PER_GROUP = 8
WIDTH = 128
TOK = 128
GROUP_CHIPS = 4
SPAN = PER_GROUP * WIDTH
ADAPTER_SCALE = 2.0
SCORE_SCALE = 1.0 / math.sqrt(WIDTH)
EXP2_SCALE = SCORE_SCALE * math.log2(math.e)
MESH = pl.DeviceIdType.MESH
F32 = jnp.float32
BF16 = jnp.bfloat16


def dot(a, b, dims):
    return lax.dot_general(a, b, (dims, ((), ())), preferred_element_type=F32)


NT = ((1,), (1,))
NN = ((1,), (0,))


STRIP = 64
BLOCK = 2 * TOK
PAIRS = PER_GROUP // 2
ROWS = 4 * TOK


def fold(x):
    return x.reshape(x.shape[0] // 8, 8, x.shape[1])


def spread(x):
    return jnp.broadcast_to(x, (8, x.shape[1]))


def main_kernel(
    n, ndp,
    flags, q_hbm, d_hbm, k_in, v_in, sq, sv, tables,
    qgs, kvg, gat, vgat,
    q, d, table, qsend, dsend, kv,
    qb, db, kvb, st, stb, kT, psend, rbuf, dqb, own,
    vpart, msg, zr, zsum, dr, res, vres,
    score, dprob, low_p, low_ds, dqT, top, total, mixed,
    loads, kvs, kvr, qs, qr, ss, sr, ps, pr, dqs, dqr,
    zs_s, zr_s, ds_s, dr_s, as_s, ar_s, vr_s,
):
    nz = n // 2
    wide = 2 * SPAN // nz
    me = lax.axis_index("ctx")
    dpi = lax.axis_index("dp")
    z = me // 2
    c = me % 2
    other = 1 - c
    sib = z * 2 + other

    def slot(us, zz):
        return (zz + 2 * us) % GROUP_CHIPS

    def copy(src, dst, send, recv, target):
        return pltpu.make_async_remote_copy(
            src_ref=src, dst_ref=dst, send_sem=send, recv_sem=recv,
            device_id=target, device_id_type=MESH,
        )

    load_q = pltpu.make_async_copy(q_hbm, q, loads.at[0])
    load_d = pltpu.make_async_copy(d_hbm, d, loads.at[1])
    load_t = pltpu.make_async_copy(tables.at[z], table, loads.at[2])
    load_q.start()
    load_d.start()
    load_t.start()

    barrier = pltpu.get_barrier_semaphore()

    @pl.loop(1, n)
    def _(o):
        pl.semaphore_signal(barrier, inc=1, device_id=(dpi, (me + o) % n), device_id_type=MESH)

    @pl.loop(1, ndp)
    def _(o):
        pl.semaphore_signal(barrier, inc=1, device_id=((dpi + o) % ndp, me), device_id_type=MESH)

    flag = [flags[h] for h in range(KV_HEADS)]

    def same(a, b):
        return 1 - (a - b) * (a - b)

    rank = [sum((same(flag[j], flag[h]) for j in range(h)), jnp.int32(0)) for h in range(KV_HEADS)]

    def share(h, cc, us):
        return (same(rank[h], cc) * same(flag[h], us)).astype(F32)

    def pick(parts, weights):
        total = None
        for part, weight in zip(parts, weights):
            term = part * jnp.full(part.shape, weight, F32).astype(part.dtype)
            total = term if total is None else total + term
        return total

    def gather(ref, width, cc, us):
        heads = range(KV_HEADS)
        return pick([ref[:, h * width : (h + 1) * width] for h in heads], [share(h, cc, us) for h in heads])

    st[...] = jnp.concatenate([sq[...].astype(F32), sv[...].astype(F32)], axis=0).astype(BF16)
    stb[0, c] = st[...]
    for s in range(KV_HEADS):
        kv[s, 0] = gather(k_in, WIDTH, s // 2, s % 2)
        kv[s, 1] = gather(v_in, WIDTH, s // 2, s % 2)
    early = (z // 2) % 2
    for us in range(2):
        kvb[us, 0, c] = kv[2 * c + us]

    pl.semaphore_wait(barrier, n - 1 + ndp - 1)

    def near_kv(us):
        return copy(kv.at[2 * other + us], kvb.at[us, 0, c], kvs.at[us, 0, other], kvr.at[us, 0, c], (dpi, sib))

    def far_kv(us, t, cc):
        zt = (z + t) % nz
        return copy(kv.at[2 * cc + us], kvb.at[us, t, c], kvs.at[us, t, cc], kvr.at[us, t, c], (dpi, 2 * zt + cc))

    def near_rows(us, i):
        src, dst = ((qsend, qb), (dsend, db))[i]
        return copy(src.at[us], dst.at[us, c], qs.at[us, i], qr.at[us, i], (dpi, sib))

    def near_state():
        return copy(st, stb.at[0, c], ss.at[0, other], sr.at[0, c], (dpi, sib))

    def far_state(t, cc):
        zt = (z + t) % nz
        return copy(st, stb.at[t, c], ss.at[t, cc], sr.at[t, c], (dpi, 2 * zt + cc))

    def far_part(us, t, h):
        zo = (z - t + nz) % nz
        return copy(psend.at[us, t, h], rbuf.at[us, t, c], ps.at[us, t, h], pr.at[us, t, c], (dpi, 2 * zo + h))

    def near_part(us):
        return copy(psend.at[us, 0, other], rbuf.at[us, 0, c], ps.at[us, 0, other], pr.at[us, 0, c], (dpi, sib))

    def near_dq(us):
        return copy(dqb.at[us, other], qgs.at[2 * c + us], dqs.at[us], dqr.at[us], (dpi, sib))

    @pl.loop(0, 2)
    def _(step):
        us = (step + early) % 2

        @pl.loop(1, GROUP_CHIPS)
        def _(t):
            @pl.when(t <= slot(us, (z + t) % nz))
            def _():
                far_kv(us, t, 0).start()
                far_kv(us, t, 1).start()

        near_kv(us).start()

    load_q.wait()
    load_d.wait()

    @pl.loop(0, 2)
    def _(step):
        us = (step + early) % 2
        qsend[us] = gather(q, SPAN, other, us)
        near_rows(us, 0).start()
        dsend[us] = gather(d, SPAN, other, us)
        near_rows(us, 1).start()
        qb[us, c] = gather(q, SPAN, c, us)
        db[us, c] = gather(d, SPAN, c, us)

    near_state().start()

    @pl.loop(1, GROUP_CHIPS)
    def _(t):
        far_state(t, 0).start()
        far_state(t, 1).start()

    load_t.wait()

    @pl.loop(0, 2)
    def _(step):
        us = (step + early) % 2
        nb = slot(us, z) + 1
        copy(kv.at[0], kvb.at[us, 0, other], kvs.at[us, 0, other], kvr.at[us, 0, other], (dpi, sib)).wait_recv()
        near_rows(us, 0).wait_recv()
        near_rows(us, 1).wait_recv()
        for pair in range(PAIRS):
            top[pair] = jnp.full((8, ROWS), -jnp.inf, F32)
            total[pair] = jnp.zeros((8, ROWS), F32)
            mixed[pair] = jnp.zeros((8, ROWS), F32)

        def rows(ref, pair):
            heads = [slice((2 * pair + g) * WIDTH, (2 * pair + g + 1) * WIDTH) for g in range(2)]
            return jnp.concatenate([ref[us, h, :, heads[g]] for g in range(2) for h in range(2)], axis=0)

        @pl.loop(0, nb)
        def _(t):
            @pl.when(t > 0)
            def _():
                for h in range(2):
                    copy(kv.at[0], kvb.at[us, t, h], kvs.at[us, t, h], kvr.at[us, t, h], (dpi, sib)).wait_recv()

            key = kvb[us, t, :, 0].reshape(BLOCK, WIDTH)
            val = kvb[us, t, :, 1].reshape(BLOCK, WIDTH)
            at = pl.ds(pl.multiple_of(t * BLOCK, BLOCK), BLOCK)
            kT[:, at] = key.astype(F32).T.astype(BF16)
            kpos = lax.broadcasted_iota(jnp.int32, (BLOCK, ROWS), 0)
            rpos = lax.broadcasted_iota(jnp.int32, (BLOCK, ROWS), 1) & (BLOCK - 1)
            seen = kpos <= rpos + t * BLOCK
            for pair in range(PAIRS):
                s = jnp.where(seen, dot(key, rows(qb, pair), NT), -jnp.inf)
                score[pair, t] = s
                top[pair] = jnp.maximum(top[pair], jnp.max(fold(s), axis=0))
                dprob[pair, t] = dot(val, rows(db, pair), NT)

        for pair in range(PAIRS):
            top[pair] = spread(jnp.max(top[pair], axis=0, keepdims=True))

        @pl.loop(0, nb)
        def _(t):
            for pair in range(PAIRS):
                high = top[pair]
                sum_w = total[pair]
                sum_m = mixed[pair]
                for i in range(0, BLOCK, STRIP):
                    at = slice(i, i + STRIP)
                    weight = jnp.exp2((fold(score[pair, t, at]) - high) * EXP2_SCALE)
                    score[pair, t, at] = weight.reshape(STRIP, ROWS)
                    sum_w = sum_w + jnp.sum(weight, axis=0)
                    sum_m = sum_m + jnp.sum(weight * fold(dprob[pair, t, at]), axis=0)
                total[pair] = sum_w
                mixed[pair] = sum_m

        for pair in range(PAIRS):
            inverse = 1.0 / jnp.sum(total[pair], axis=0, keepdims=True)
            delta = jnp.sum(mixed[pair], axis=0, keepdims=True) * inverse
            total[pair] = spread(inverse)
            mixed[pair] = spread(delta)

        @pl.loop(0, nb)
        def _(back):
            t = nb - 1 - back
            dk = jnp.zeros((BLOCK, WIDTH), F32)
            dv = jnp.zeros((BLOCK, WIDTH), F32)
            for pair in range(PAIRS):
                inverse = total[pair]
                delta = mixed[pair]
                for i in range(0, BLOCK, STRIP):
                    at = slice(i, i + STRIP)
                    prob = fold(score[pair, t, at]) * inverse
                    ds = prob * (fold(dprob[pair, t, at]) - delta)
                    low_p[pair, at] = prob.reshape(STRIP, ROWS).astype(BF16)
                    low_ds[pair, t, at] = ds.reshape(STRIP, ROWS).astype(BF16)
                dv = dv + dot(low_p[pair], rows(db, pair), NN)
                dk = dk + dot(low_ds[pair, t], rows(qb, pair), NN)
            for h in range(2):
                psend[us, t, h, 0] = dk[h * TOK : (h + 1) * TOK].astype(BF16)
                psend[us, t, h, 1] = dv[h * TOK : (h + 1) * TOK].astype(BF16)

            @pl.when(t > 0)
            def _():
                far_part(us, t, 0).start()
                far_part(us, t, 1).start()

        near_part(us).start()

        for count in range(1, GROUP_CHIPS + 1):
            @pl.when(nb == count)
            def _(count=count):
                for pair in range(PAIRS):
                    ds = low_ds[pair, 0:count].reshape(count * BLOCK, ROWS)
                    dqT[pair] = dot(kT[:, : count * BLOCK], ds, NN)

        cos = jnp.concatenate([table[0], table[0]], axis=1)
        sin = jnp.concatenate([table[1], table[1]], axis=1)
        for pair in range(PAIRS):
            front = dqT[pair, : WIDTH // 2] * SCORE_SCALE
            back = dqT[pair, WIDTH // 2 :] * SCORE_SCALE
            turned = jnp.concatenate([front * cos + back * sin, back * cos - front * sin], axis=0)
            dq = turned.T.astype(BF16)
            for g in range(2):
                for h in range(2):
                    at = (g * 2 + h) * TOK
                    dqb[us, h, :, (2 * pair + g) * WIDTH : (2 * pair + g + 1) * WIDTH] = dq[at : at + TOK]
        near_dq(us).start()

        @pl.when(step == 0)
        def _():
            copy(st, stb.at[0, other], ss.at[0, other], sr.at[0, other], (dpi, sib)).wait_recv()

            @pl.loop(1, GROUP_CHIPS)
            def _(t):
                for h in range(2):
                    copy(st, stb.at[t, h], ss.at[t, h], sr.at[t, h], (dpi, sib)).wait_recv()

        part = dot(stb[0, 0], dqb[us, 0], NN) + dot(stb[0, 1], dqb[us, 1], NN)
        for j in range(nz // 2):
            msg[us * (nz // 2) + j, :, :wide] = part[:8, j * wide : (j + 1) * wide]

        def value_term(t, x):
            return x + dot(stb[t, 0], psend[us, t, 0, 1], NN) + dot(stb[t, 1], psend[us, t, 1, 1], NN)

        vpart[us] = lax.fori_loop(0, nb, value_term, jnp.zeros((16, WIDTH), F32))
        rbuf[us, 0, c] = psend[us, 0, c]
        qgs[2 * c + us] = dqb[us, c]

    for k in range(nz):
        for us in range(2):
            msg[k, :, wide + us * WIDTH : wide + (us + 1) * WIDTH] = vpart[us, 8:]

    def to_chip(k):
        return copy(msg.at[k], zr.at[z], zs_s.at[k], zr_s.at[z], (dpi, 2 * k + c))

    @pl.loop(1, nz)
    def _(o):
        to_chip((z + o) % nz).start()

    zr[z] = msg[z]

    @pl.loop(1, nz)
    def _(o):
        k = (z + o) % nz
        copy(msg.at[k], zr.at[k], zs_s.at[k], zr_s.at[k], (dpi, sib)).wait_recv()

    zsum[...] = lax.fori_loop(0, nz, lambda k, x: x + zr[k], jnp.zeros((8, wide + 2 * WIDTH), F32))

    def to_dp(o):
        return copy(zsum, dr.at[dpi], ds_s.at[o], dr_s.at[dpi], ((dpi + o) % ndp, me))

    @pl.loop(1, ndp)
    def _(o):
        to_dp(o).start()

    dr[dpi] = zsum[...]

    def owner_sum(us):
        copy(kv.at[0], rbuf.at[us, 0, other], ps.at[us, 0, other], pr.at[us, 0, other], (dpi, sib)).wait_recv()
        for cc in range(2):
            own[us, cc] = rbuf[us, 0, cc].astype(F32)

        @pl.loop(1, GROUP_CHIPS)
        def _(t):
            @pl.when(t <= slot(us, (z + t) % nz))
            def _():
                for cc in range(2):
                    copy(kv.at[0], rbuf.at[us, t, cc], ps.at[us, t, cc], pr.at[us, t, cc], (dpi, sib)).wait_recv()
                    own[us, cc] += rbuf[us, t, cc].astype(F32)

    @pl.loop(1, ndp)
    def _(o):
        k = (dpi + o) % ndp
        copy(zsum, dr.at[k], ds_s.at[o], dr_s.at[k], (dpi, sib)).wait_recv()

    summed = (
        lax.fori_loop(0, ndp, lambda k, x: x + dr[k], jnp.zeros((8, wide + 2 * WIDTH), F32)) * ADAPTER_SCALE
    )
    res[...] = summed[:, :wide]
    vres[...] = summed[:, wide:]

    def to_ctx(o):
        return copy(res, gat.at[me], as_s.at[o], ar_s.at[me], (dpi, (me + o) % n))

    def to_sib():
        return copy(vres, vgat.at[c], as_s.at[0], vr_s, (dpi, sib))

    to_sib().start()

    @pl.loop(1, n)
    def _(o):
        to_ctx(o).start()

    gat[me] = res[...]
    vgat[c] = vres[...]

    @pl.loop(0, 2)
    def _(us):
        copy(dqb.at[us, other], qgs.at[2 * other + us], dqs.at[us], dqr.at[us], (dpi, sib)).wait_recv()

    @pl.loop(0, 2)
    def _(us):
        owner_sum(us)

    cos = jnp.where(c == 0, table[0, :, :TOK], table[0, :, TOK:]).T
    sin = jnp.where(c == 0, table[1, :, :TOK], table[1, :, TOK:]).T
    cos = jnp.concatenate([cos, cos], axis=1)
    sin = jnp.concatenate([sin, -sin], axis=1)
    for cc in range(2):
        for us in range(2):
            dk = own[us, cc, 0] * SCORE_SCALE
            kvg[2 * cc + us, 0] = (dk * cos + pltpu.roll(dk, WIDTH // 2, 1) * sin).astype(BF16)
            kvg[2 * cc + us, 1] = own[us, cc, 1].astype(BF16)

    @pl.loop(1, n)
    def _(o):
        k = (me + o) % n
        copy(res, gat.at[k], as_s.at[o], ar_s.at[k], (dpi, sib)).wait_recv()

    copy(vres, vgat.at[other], as_s.at[0], vr_s, (dpi, sib)).wait_recv()
    to_sib().wait_send()

    @pl.loop(0, 2)
    def _(us):
        near_dq(us).wait_send()
        near_kv(us).wait_send()
        near_rows(us, 0).wait_send()
        near_rows(us, 1).wait_send()
        near_part(us).wait_send()

        @pl.loop(1, GROUP_CHIPS)
        def _(t):
            @pl.when(t <= slot(us, (z + t) % nz))
            def _():
                far_kv(us, t, 0).wait_send()
                far_kv(us, t, 1).wait_send()

            @pl.when(t <= slot(us, z))
            def _():
                far_part(us, t, 0).wait_send()
                far_part(us, t, 1).wait_send()

    near_state().wait_send()

    @pl.loop(1, GROUP_CHIPS)
    def _(t):
        far_state(t, 0).wait_send()
        far_state(t, 1).wait_send()

    @pl.loop(1, nz)
    def _(o):
        to_chip((z + o) % nz).wait_send()

    @pl.loop(1, ndp)
    def _(o):
        to_dp(o).wait_send()

    @pl.loop(1, n)
    def _(o):
        to_ctx(o).wait_send()


def main_call(n, ndp, *operands):
    nz = n // 2
    line = 2 * SPAN // nz + 2 * WIDTH
    vmem = pl.BlockSpec(memory_space=pltpu.VMEM)
    smem = pl.BlockSpec(memory_space=pltpu.SMEM)
    away = pl.BlockSpec(memory_space=pl.ANY)
    dma = pltpu.SemaphoreType.DMA
    return pl.pallas_call(
        functools.partial(main_kernel, n, ndp),
        in_specs=[smem, away, away, vmem, vmem, vmem, vmem, away],
        out_specs=[vmem] * 4,
        out_shape=[
            jax.ShapeDtypeStruct((KV_HEADS, TOK, SPAN), BF16),
            jax.ShapeDtypeStruct((KV_HEADS, 2, TOK, WIDTH), BF16),
            jax.ShapeDtypeStruct((n, 8, line - 2 * WIDTH), F32),
            jax.ShapeDtypeStruct((2, 8, 2 * WIDTH), F32),
        ],
        scratch_shapes=[
            pltpu.VMEM((TOK, KV_HEADS * SPAN), BF16),
            pltpu.VMEM((TOK, KV_HEADS * SPAN), BF16),
            pltpu.VMEM((2, WIDTH // 2, 2 * TOK), F32),
            pltpu.VMEM((2, TOK, SPAN), BF16),
            pltpu.VMEM((2, TOK, SPAN), BF16),
            pltpu.VMEM((KV_HEADS, 2, TOK, WIDTH), BF16),
            pltpu.VMEM((2, 2, TOK, SPAN), BF16),
            pltpu.VMEM((2, 2, TOK, SPAN), BF16),
            pltpu.VMEM((2, GROUP_CHIPS, 2, 2, TOK, WIDTH), BF16),
            pltpu.VMEM((16, TOK), BF16),
            pltpu.VMEM((GROUP_CHIPS, 2, 16, TOK), BF16),
            pltpu.VMEM((WIDTH, GROUP_CHIPS * 2 * TOK), BF16),
            pltpu.VMEM((2, GROUP_CHIPS, 2, 2, TOK, WIDTH), BF16),
            pltpu.VMEM((2, GROUP_CHIPS, 2, 2, TOK, WIDTH), BF16),
            pltpu.VMEM((2, 2, TOK, SPAN), BF16),
            pltpu.VMEM((2, 2, 2, TOK, WIDTH), F32),
            pltpu.VMEM((2, 16, WIDTH), F32),
            pltpu.VMEM((nz, 8, line), F32),
            pltpu.VMEM((nz, 8, line), F32),
            pltpu.VMEM((8, line), F32),
            pltpu.VMEM((ndp, 8, line), F32),
            pltpu.VMEM((8, line - 2 * WIDTH), F32),
            pltpu.VMEM((8, 2 * WIDTH), F32),
            pltpu.VMEM((PAIRS, GROUP_CHIPS, BLOCK, ROWS), F32),
            pltpu.VMEM((PAIRS, GROUP_CHIPS, BLOCK, ROWS), F32),
            pltpu.VMEM((PAIRS, BLOCK, ROWS), BF16),
            pltpu.VMEM((PAIRS, GROUP_CHIPS, BLOCK, ROWS), BF16),
            pltpu.VMEM((PAIRS, WIDTH, ROWS), F32),
            pltpu.VMEM((PAIRS, 8, ROWS), F32),
            pltpu.VMEM((PAIRS, 8, ROWS), F32),
            pltpu.VMEM((PAIRS, 8, ROWS), F32),
            dma((3,)),
            dma((2, GROUP_CHIPS, 2)), dma((2, GROUP_CHIPS, 2)),
            dma((2, 2)), dma((2, 2)),
            dma((GROUP_CHIPS, 2)), dma((GROUP_CHIPS, 2)),
            dma((2, GROUP_CHIPS, 2)), dma((2, GROUP_CHIPS, 2)),
            dma((2,)), dma((2,)),
            dma((nz,)), dma((nz,)),
            dma((ndp,)), dma((ndp,)),
            dma((n,)), dma((n,)), dma,
        ],
        compiler_params=pltpu.CompilerParams(
            collective_id=0, has_side_effects=True, vmem_limit_bytes=56 * 1024 * 1024
        ),
        name="attention_backward",
    )(*operands)


def restore_kernel(n, flags, qgs, kvg, gat, vgat, qg, kg, vg, qa, va):
    nz = n // 2
    wide = 2 * SPAN // nz
    for h in range(KV_HEADS):
        us = flags[h]
        cc = sum((jnp.where(flags[j] == us, 1, 0) for j in range(h)), jnp.int32(0))
        qg[:, h * SPAN : (h + 1) * SPAN] = qgs[2 * cc + us]
        kg[:, h * WIDTH : (h + 1) * WIDTH] = kvg[2 * cc + us, 0]
        vg[:, h * WIDTH : (h + 1) * WIDTH] = kvg[2 * cc + us, 1]
        for j in range(nz // 2):
            at = h * SPAN + j * wide
            qa[:, at : at + wide] = gat[2 * (us * (nz // 2) + j) + cc]
        at = pl.ds(pl.multiple_of(us * WIDTH, WIDTH), WIDTH)
        va[:, h * WIDTH : (h + 1) * WIDTH] = vgat[cc, :, at]


def restore(n, flags, *operands):
    vmem = pl.BlockSpec(memory_space=pltpu.VMEM)
    hw = KV_HEADS * WIDTH
    return pl.pallas_call(
        functools.partial(restore_kernel, n),
        in_specs=[pl.BlockSpec(memory_space=pltpu.SMEM)] + [vmem] * 4,
        out_specs=[vmem] * 5,
        out_shape=[
            jax.ShapeDtypeStruct((TOK, KV_HEADS * SPAN), BF16),
            jax.ShapeDtypeStruct((TOK, hw), BF16),
            jax.ShapeDtypeStruct((TOK, hw), BF16),
            jax.ShapeDtypeStruct((8, KV_HEADS * SPAN), F32),
            jax.ShapeDtypeStruct((8, hw), F32),
        ],
        compiler_params=pltpu.CompilerParams(vmem_limit_bytes=56 * 1024 * 1024),
        name="restore_heads",
    )(flags, *operands)


def position_tables(n):
    half = WIDTH // 2
    inv_freq = 10000.0 ** (-(np.arange(half) * 2.0) / WIDTH)
    angle = inv_freq[None, :, None] * np.arange(n * TOK).reshape(n // 2, 1, 2 * TOK)
    return np.stack([np.cos(angle), np.sin(angle)], axis=1).astype(np.float32)


def local(n, ndp, query, keys, values, out_grad, query_state, value_state, flags):
    tables = jnp.asarray(position_tables(n))
    places = main_call(
        n, ndp, flags, query[0], out_grad[0], keys[0], values[0], query_state[0].T, value_state[0].T, tables
    )
    qg, kg, vg, qa, va = restore(n, flags, *places)
    return qg[None], kg[None], vg[None], qa, va


def solution(mesh):
    split = P("dp", "ctx", None)
    return jax.shard_map(
        functools.partial(local, mesh.shape["ctx"], mesh.shape["dp"]),
        mesh=mesh,
        in_specs=(split,) * 6 + (P(),),
        out_specs=(split, split, split, P(), P()),
        check_vma=False,
    )
```

```python
import functools
import math

import jax
import jax.numpy as jnp
from jax import lax
from jax.experimental import pallas as pl
from jax.experimental.pallas import tpu as pltpu
from jax.sharding import PartitionSpec as P
import numpy as np

KV_HEADS = 4
PER_GROUP = 8
WIDTH = 128
TOK = 128
GROUP_CHIPS = 4
SPAN = PER_GROUP * WIDTH
ADAPTER_SCALE = 2.0
SCORE_SCALE = 1.0 / math.sqrt(WIDTH)
EXP2_SCALE = SCORE_SCALE * math.log2(math.e)
MESH = pl.DeviceIdType.MESH
F32 = jnp.float32
BF16 = jnp.bfloat16


def dot(a, b, dims):
    return lax.dot_general(a, b, (dims, ((), ())), preferred_element_type=F32)


NT = ((1,), (1,))
NN = ((1,), (0,))


STRIP = 64
BLOCK = 2 * TOK
PAIRS = PER_GROUP // 2
ROWS = 4 * TOK


def fold(x):
    return x.reshape(x.shape[0] // 8, 8, x.shape[1])


def spread(x):
    return jnp.broadcast_to(x, (8, x.shape[1]))


def main_kernel(
    n, ndp,
    flags, q_hbm, d_hbm, k_in, v_in, sq, sv, tables,
    qgs, kvg, gat, vgat,
    q, d, table, qsend, dsend, kv,
    qb, db, kvb, st, stb, kT, psend, rbuf, dqb, own,
    vpart, msg, zr, zsum, dr, res, vres,
    score, dprob, low_p, low_ds, dqT, top, total, mixed,
    loads, kvs, kvr, qs, qr, ss, sr, ps, pr, dqs, dqr,
    zs_s, zr_s, ds_s, dr_s, as_s, ar_s, vr_s,
):
    nz = n // 2
    wide = 2 * SPAN // nz
    me = lax.axis_index("ctx")
    dpi = lax.axis_index("dp")
    z = me // 2
    c = me % 2
    other = 1 - c
    sib = z * 2 + other

    def slot(us, zz):
        return (zz + 2 * us) % GROUP_CHIPS

    def copy(src, dst, send, recv, target):
        return pltpu.make_async_remote_copy(
            src_ref=src, dst_ref=dst, send_sem=send, recv_sem=recv,
            device_id=target, device_id_type=MESH,
        )

    load_q = pltpu.make_async_copy(q_hbm, q, loads.at[0])
    load_d = pltpu.make_async_copy(d_hbm, d, loads.at[1])
    load_t = pltpu.make_async_copy(tables.at[z], table, loads.at[2])
    load_q.start()
    load_d.start()
    load_t.start()

    barrier = pltpu.get_barrier_semaphore()

    @pl.loop(1, n)
    def _(o):
        pl.semaphore_signal(barrier, inc=1, device_id=(dpi, (me + o) % n), device_id_type=MESH)

    @pl.loop(1, ndp)
    def _(o):
        pl.semaphore_signal(barrier, inc=1, device_id=((dpi + o) % ndp, me), device_id_type=MESH)

    flag = [flags[h] for h in range(KV_HEADS)]

    def same(a, b):
        return 1 - (a - b) * (a - b)

    rank = [sum((same(flag[j], flag[h]) for j in range(h)), jnp.int32(0)) for h in range(KV_HEADS)]

    def share(h, cc, us):
        return (same(rank[h], cc) * same(flag[h], us)).astype(F32)

    def pick(parts, weights):
        total = None
        for part, weight in zip(parts, weights):
            term = part * jnp.full(part.shape, weight, F32).astype(part.dtype)
            total = term if total is None else total + term
        return total

    def gather(ref, width, cc, us):
        heads = range(KV_HEADS)
        return pick([ref[:, h * width : (h + 1) * width] for h in heads], [share(h, cc, us) for h in heads])

    st[...] = jnp.concatenate([sq[...].astype(F32), sv[...].astype(F32)], axis=0).astype(BF16)
    stb[0, c] = st[...]
    for s in range(KV_HEADS):
        kv[s, 0] = gather(k_in, WIDTH, s // 2, s % 2)
        kv[s, 1] = gather(v_in, WIDTH, s // 2, s % 2)
    early = (z // 2) % 2
    large = 1 - early
    for us in range(2):
        kvb[us, 0, c] = kv[2 * c + us]

    pl.semaphore_wait(barrier, n - 1 + ndp - 1)

    def near_kv(us):
        return copy(kv.at[2 * other + us], kvb.at[us, 0, c], kvs.at[us, 0, other], kvr.at[us, 0, c], (dpi, sib))

    def far_kv(us, t, cc):
        zt = (z + t) % nz
        return copy(kv.at[2 * cc + us], kvb.at[us, t, c], kvs.at[us, t, cc], kvr.at[us, t, c], (dpi, 2 * zt + cc))

    def near_rows(us, i):
        src, dst = ((qsend, qb), (dsend, db))[i]
        return copy(src.at[us], dst.at[us, c], qs.at[us, i], qr.at[us, i], (dpi, sib))

    def near_state():
        return copy(st, stb.at[0, c], ss.at[0, other], sr.at[0, c], (dpi, sib))

    def far_state(t, cc):
        zt = (z + t) % nz
        return copy(st, stb.at[t, c], ss.at[t, cc], sr.at[t, c], (dpi, 2 * zt + cc))

    def far_part(us, t, h):
        zo = (z - t + nz) % nz
        return copy(psend.at[us, t, h], rbuf.at[us, t, c], ps.at[us, t, h], pr.at[us, t, c], (dpi, 2 * zo + h))

    def near_part(us):
        return copy(psend.at[us, 0, other], rbuf.at[us, 0, c], ps.at[us, 0, other], pr.at[us, 0, c], (dpi, sib))

    def near_dq(us):
        return copy(dqb.at[us, other], qgs.at[2 * c + us], dqs.at[us], dqr.at[us], (dpi, sib))

    @pl.loop(0, 2)
    def _(step):
        us = (step + early) % 2

        @pl.loop(1, GROUP_CHIPS)
        def _(t):
            @pl.when(t <= slot(us, (z + t) % nz))
            def _():
                far_kv(us, t, 0).start()
                far_kv(us, t, 1).start()

        near_kv(us).start()

    load_q.wait()
    load_d.wait()

    @pl.loop(0, 2)
    def _(step):
        us = (step + large) % 2
        qsend[us] = gather(q, SPAN, other, us)
        near_rows(us, 0).start()
        dsend[us] = gather(d, SPAN, other, us)
        near_rows(us, 1).start()
        qb[us, c] = gather(q, SPAN, c, us)
        db[us, c] = gather(d, SPAN, c, us)

    near_state().start()

    @pl.loop(1, GROUP_CHIPS)
    def _(t):
        far_state(t, 0).start()
        far_state(t, 1).start()

    load_t.wait()

    @pl.loop(0, 2)
    def _(step):
        us = (step + large) % 2
        nb = slot(us, z) + 1
        copy(kv.at[0], kvb.at[us, 0, other], kvs.at[us, 0, other], kvr.at[us, 0, other], (dpi, sib)).wait_recv()
        near_rows(us, 0).wait_recv()
        near_rows(us, 1).wait_recv()
        for pair in range(PAIRS):
            top[pair] = jnp.full((8, ROWS), -jnp.inf, F32)
            total[pair] = jnp.zeros((8, ROWS), F32)
            mixed[pair] = jnp.zeros((8, ROWS), F32)

        def rows(ref, pair):
            heads = [slice((2 * pair + g) * WIDTH, (2 * pair + g + 1) * WIDTH) for g in range(2)]
            return jnp.concatenate([ref[us, h, :, heads[g]] for g in range(2) for h in range(2)], axis=0)

        @pl.loop(0, nb)
        def _(t):
            @pl.when(t > 0)
            def _():
                for h in range(2):
                    copy(kv.at[0], kvb.at[us, t, h], kvs.at[us, t, h], kvr.at[us, t, h], (dpi, sib)).wait_recv()

            key = kvb[us, t, :, 0].reshape(BLOCK, WIDTH)
            val = kvb[us, t, :, 1].reshape(BLOCK, WIDTH)
            at = pl.ds(pl.multiple_of(t * BLOCK, BLOCK), BLOCK)
            kT[:, at] = key.astype(F32).T.astype(BF16)
            kpos = lax.broadcasted_iota(jnp.int32, (BLOCK, ROWS), 0)
            rpos = lax.broadcasted_iota(jnp.int32, (BLOCK, ROWS), 1) & (BLOCK - 1)
            seen = kpos <= rpos + t * BLOCK
            for pair in range(PAIRS):
                s = jnp.where(seen, dot(key, rows(qb, pair), NT), -jnp.inf)
                score[pair, t] = s
                top[pair] = jnp.maximum(top[pair], jnp.max(fold(s), axis=0))
                dprob[pair, t] = dot(val, rows(db, pair), NT)

        for pair in range(PAIRS):
            top[pair] = spread(jnp.max(top[pair], axis=0, keepdims=True))

        @pl.loop(0, nb)
        def _(t):
            for pair in range(PAIRS):
                high = top[pair]
                sum_w = total[pair]
                sum_m = mixed[pair]
                for i in range(0, BLOCK, STRIP):
                    at = slice(i, i + STRIP)
                    weight = jnp.exp2((fold(score[pair, t, at]) - high) * EXP2_SCALE)
                    score[pair, t, at] = weight.reshape(STRIP, ROWS)
                    sum_w = sum_w + jnp.sum(weight, axis=0)
                    sum_m = sum_m + jnp.sum(weight * fold(dprob[pair, t, at]), axis=0)
                total[pair] = sum_w
                mixed[pair] = sum_m

        for pair in range(PAIRS):
            inverse = 1.0 / jnp.sum(total[pair], axis=0, keepdims=True)
            delta = jnp.sum(mixed[pair], axis=0, keepdims=True) * inverse
            total[pair] = spread(inverse)
            mixed[pair] = spread(delta)

        @pl.loop(0, nb)
        def _(back):
            t = nb - 1 - back
            dk = jnp.zeros((BLOCK, WIDTH), F32)
            dv = jnp.zeros((BLOCK, WIDTH), F32)
            for pair in range(PAIRS):
                inverse = total[pair]
                delta = mixed[pair]
                for i in range(0, BLOCK, STRIP):
                    at = slice(i, i + STRIP)
                    prob = fold(score[pair, t, at]) * inverse
                    ds = prob * (fold(dprob[pair, t, at]) - delta)
                    low_p[pair, at] = prob.reshape(STRIP, ROWS).astype(BF16)
                    low_ds[pair, t, at] = ds.reshape(STRIP, ROWS).astype(BF16)
                dv = dv + dot(low_p[pair], rows(db, pair), NN)
                dk = dk + dot(low_ds[pair, t], rows(qb, pair), NN)
            for h in range(2):
                psend[us, t, h, 0] = dk[h * TOK : (h + 1) * TOK].astype(BF16)
                psend[us, t, h, 1] = dv[h * TOK : (h + 1) * TOK].astype(BF16)

            @pl.when(t > 0)
            def _():
                far_part(us, t, 0).start()
                far_part(us, t, 1).start()

        near_part(us).start()

        for count in range(1, GROUP_CHIPS + 1):
            @pl.when(nb == count)
            def _(count=count):
                for pair in range(PAIRS):
                    ds = low_ds[pair, 0:count].reshape(count * BLOCK, ROWS)
                    dqT[pair] = dot(kT[:, : count * BLOCK], ds, NN)

        cos = jnp.concatenate([table[0], table[0]], axis=1)
        sin = jnp.concatenate([table[1], table[1]], axis=1)
        for pair in range(PAIRS):
            front = dqT[pair, : WIDTH // 2] * SCORE_SCALE
            back = dqT[pair, WIDTH // 2 :] * SCORE_SCALE
            turned = jnp.concatenate([front * cos + back * sin, back * cos - front * sin], axis=0)
            dq = turned.T.astype(BF16)
            for g in range(2):
                for h in range(2):
                    at = (g * 2 + h) * TOK
                    dqb[us, h, :, (2 * pair + g) * WIDTH : (2 * pair + g + 1) * WIDTH] = dq[at : at + TOK]
        near_dq(us).start()

        @pl.when(step == 0)
        def _():
            copy(st, stb.at[0, other], ss.at[0, other], sr.at[0, other], (dpi, sib)).wait_recv()

            @pl.loop(1, GROUP_CHIPS)
            def _(t):
                for h in range(2):
                    copy(st, stb.at[t, h], ss.at[t, h], sr.at[t, h], (dpi, sib)).wait_recv()

        part = dot(stb[0, 0], dqb[us, 0], NN) + dot(stb[0, 1], dqb[us, 1], NN)
        for j in range(nz // 2):
            msg[us * (nz // 2) + j, :, :wide] = part[:8, j * wide : (j + 1) * wide]

        def value_term(t, x):
            return x + dot(stb[t, 0], psend[us, t, 0, 1], NN) + dot(stb[t, 1], psend[us, t, 1, 1], NN)

        vpart[us] = lax.fori_loop(0, nb, value_term, jnp.zeros((16, WIDTH), F32))
        rbuf[us, 0, c] = psend[us, 0, c]
        qgs[2 * c + us] = dqb[us, c]

    for k in range(nz):
        for us in range(2):
            msg[k, :, wide + us * WIDTH : wide + (us + 1) * WIDTH] = vpart[us, 8:]

    def to_chip(k):
        return copy(msg.at[k], zr.at[z], zs_s.at[k], zr_s.at[z], (dpi, 2 * k + c))

    @pl.loop(1, nz)
    def _(o):
        to_chip((z + o) % nz).start()

    zr[z] = msg[z]

    @pl.loop(1, nz)
    def _(o):
        k = (z + o) % nz
        copy(msg.at[k], zr.at[k], zs_s.at[k], zr_s.at[k], (dpi, sib)).wait_recv()

    zsum[...] = lax.fori_loop(0, nz, lambda k, x: x + zr[k], jnp.zeros((8, wide + 2 * WIDTH), F32))

    def to_dp(o):
        return copy(zsum, dr.at[dpi], ds_s.at[o], dr_s.at[dpi], ((dpi + o) % ndp, me))

    @pl.loop(1, ndp)
    def _(o):
        to_dp(o).start()

    dr[dpi] = zsum[...]

    def owner_sum(us):
        copy(kv.at[0], rbuf.at[us, 0, other], ps.at[us, 0, other], pr.at[us, 0, other], (dpi, sib)).wait_recv()
        for cc in range(2):
            own[us, cc] = rbuf[us, 0, cc].astype(F32)

        @pl.loop(1, GROUP_CHIPS)
        def _(t):
            @pl.when(t <= slot(us, (z + t) % nz))
            def _():
                for cc in range(2):
                    copy(kv.at[0], rbuf.at[us, t, cc], ps.at[us, t, cc], pr.at[us, t, cc], (dpi, sib)).wait_recv()
                    own[us, cc] += rbuf[us, t, cc].astype(F32)

    @pl.loop(1, ndp)
    def _(o):
        k = (dpi + o) % ndp
        copy(zsum, dr.at[k], ds_s.at[o], dr_s.at[k], (dpi, sib)).wait_recv()

    summed = (
        lax.fori_loop(0, ndp, lambda k, x: x + dr[k], jnp.zeros((8, wide + 2 * WIDTH), F32)) * ADAPTER_SCALE
    )
    res[...] = summed[:, :wide]
    vres[...] = summed[:, wide:]

    def to_ctx(o):
        return copy(res, gat.at[me], as_s.at[o], ar_s.at[me], (dpi, (me + o) % n))

    def to_sib():
        return copy(vres, vgat.at[c], as_s.at[0], vr_s, (dpi, sib))

    to_sib().start()

    @pl.loop(1, n)
    def _(o):
        to_ctx(o).start()

    gat[me] = res[...]
    vgat[c] = vres[...]

    @pl.loop(0, 2)
    def _(us):
        copy(dqb.at[us, other], qgs.at[2 * other + us], dqs.at[us], dqr.at[us], (dpi, sib)).wait_recv()

    @pl.loop(0, 2)
    def _(us):
        owner_sum(us)

    cos = jnp.where(c == 0, table[0, :, :TOK], table[0, :, TOK:]).T
    sin = jnp.where(c == 0, table[1, :, :TOK], table[1, :, TOK:]).T
    cos = jnp.concatenate([cos, cos], axis=1)
    sin = jnp.concatenate([sin, -sin], axis=1)
    for cc in range(2):
        for us in range(2):
            dk = own[us, cc, 0] * SCORE_SCALE
            kvg[2 * cc + us, 0] = (dk * cos + pltpu.roll(dk, WIDTH // 2, 1) * sin).astype(BF16)
            kvg[2 * cc + us, 1] = own[us, cc, 1].astype(BF16)

    @pl.loop(1, n)
    def _(o):
        k = (me + o) % n
        copy(res, gat.at[k], as_s.at[o], ar_s.at[k], (dpi, sib)).wait_recv()

    copy(vres, vgat.at[other], as_s.at[0], vr_s, (dpi, sib)).wait_recv()
    to_sib().wait_send()

    @pl.loop(0, 2)
    def _(us):
        near_dq(us).wait_send()
        near_kv(us).wait_send()
        near_rows(us, 0).wait_send()
        near_rows(us, 1).wait_send()
        near_part(us).wait_send()

        @pl.loop(1, GROUP_CHIPS)
        def _(t):
            @pl.when(t <= slot(us, (z + t) % nz))
            def _():
                far_kv(us, t, 0).wait_send()
                far_kv(us, t, 1).wait_send()

            @pl.when(t <= slot(us, z))
            def _():
                far_part(us, t, 0).wait_send()
                far_part(us, t, 1).wait_send()

    near_state().wait_send()

    @pl.loop(1, GROUP_CHIPS)
    def _(t):
        far_state(t, 0).wait_send()
        far_state(t, 1).wait_send()

    @pl.loop(1, nz)
    def _(o):
        to_chip((z + o) % nz).wait_send()

    @pl.loop(1, ndp)
    def _(o):
        to_dp(o).wait_send()

    @pl.loop(1, n)
    def _(o):
        to_ctx(o).wait_send()


def main_call(n, ndp, *operands):
    nz = n // 2
    line = 2 * SPAN // nz + 2 * WIDTH
    vmem = pl.BlockSpec(memory_space=pltpu.VMEM)
    smem = pl.BlockSpec(memory_space=pltpu.SMEM)
    away = pl.BlockSpec(memory_space=pl.ANY)
    dma = pltpu.SemaphoreType.DMA
    return pl.pallas_call(
        functools.partial(main_kernel, n, ndp),
        in_specs=[smem, away, away, vmem, vmem, vmem, vmem, away],
        out_specs=[vmem] * 4,
        out_shape=[
            jax.ShapeDtypeStruct((KV_HEADS, TOK, SPAN), BF16),
            jax.ShapeDtypeStruct((KV_HEADS, 2, TOK, WIDTH), BF16),
            jax.ShapeDtypeStruct((n, 8, line - 2 * WIDTH), F32),
            jax.ShapeDtypeStruct((2, 8, 2 * WIDTH), F32),
        ],
        scratch_shapes=[
            pltpu.VMEM((TOK, KV_HEADS * SPAN), BF16),
            pltpu.VMEM((TOK, KV_HEADS * SPAN), BF16),
            pltpu.VMEM((2, WIDTH // 2, 2 * TOK), F32),
            pltpu.VMEM((2, TOK, SPAN), BF16),
            pltpu.VMEM((2, TOK, SPAN), BF16),
            pltpu.VMEM((KV_HEADS, 2, TOK, WIDTH), BF16),
            pltpu.VMEM((2, 2, TOK, SPAN), BF16),
            pltpu.VMEM((2, 2, TOK, SPAN), BF16),
            pltpu.VMEM((2, GROUP_CHIPS, 2, 2, TOK, WIDTH), BF16),
            pltpu.VMEM((16, TOK), BF16),
            pltpu.VMEM((GROUP_CHIPS, 2, 16, TOK), BF16),
            pltpu.VMEM((WIDTH, GROUP_CHIPS * 2 * TOK), BF16),
            pltpu.VMEM((2, GROUP_CHIPS, 2, 2, TOK, WIDTH), BF16),
            pltpu.VMEM((2, GROUP_CHIPS, 2, 2, TOK, WIDTH), BF16),
            pltpu.VMEM((2, 2, TOK, SPAN), BF16),
            pltpu.VMEM((2, 2, 2, TOK, WIDTH), F32),
            pltpu.VMEM((2, 16, WIDTH), F32),
            pltpu.VMEM((nz, 8, line), F32),
            pltpu.VMEM((nz, 8, line), F32),
            pltpu.VMEM((8, line), F32),
            pltpu.VMEM((ndp, 8, line), F32),
            pltpu.VMEM((8, line - 2 * WIDTH), F32),
            pltpu.VMEM((8, 2 * WIDTH), F32),
            pltpu.VMEM((PAIRS, GROUP_CHIPS, BLOCK, ROWS), F32),
            pltpu.VMEM((PAIRS, GROUP_CHIPS, BLOCK, ROWS), F32),
            pltpu.VMEM((PAIRS, BLOCK, ROWS), BF16),
            pltpu.VMEM((PAIRS, GROUP_CHIPS, BLOCK, ROWS), BF16),
            pltpu.VMEM((PAIRS, WIDTH, ROWS), F32),
            pltpu.VMEM((PAIRS, 8, ROWS), F32),
            pltpu.VMEM((PAIRS, 8, ROWS), F32),
            pltpu.VMEM((PAIRS, 8, ROWS), F32),
            dma((3,)),
            dma((2, GROUP_CHIPS, 2)), dma((2, GROUP_CHIPS, 2)),
            dma((2, 2)), dma((2, 2)),
            dma((GROUP_CHIPS, 2)), dma((GROUP_CHIPS, 2)),
            dma((2, GROUP_CHIPS, 2)), dma((2, GROUP_CHIPS, 2)),
            dma((2,)), dma((2,)),
            dma((nz,)), dma((nz,)),
            dma((ndp,)), dma((ndp,)),
            dma((n,)), dma((n,)), dma,
        ],
        compiler_params=pltpu.CompilerParams(
            collective_id=0, has_side_effects=True, vmem_limit_bytes=56 * 1024 * 1024
        ),
        name="attention_backward",
    )(*operands)


def restore_kernel(n, flags, qgs, kvg, gat, vgat, qg, kg, vg, qa, va):
    nz = n // 2
    wide = 2 * SPAN // nz
    for h in range(KV_HEADS):
        us = flags[h]
        cc = sum((jnp.where(flags[j] == us, 1, 0) for j in range(h)), jnp.int32(0))
        qg[:, h * SPAN : (h + 1) * SPAN] = qgs[2 * cc + us]
        kg[:, h * WIDTH : (h + 1) * WIDTH] = kvg[2 * cc + us, 0]
        vg[:, h * WIDTH : (h + 1) * WIDTH] = kvg[2 * cc + us, 1]
        for j in range(nz // 2):
            at = h * SPAN + j * wide
            qa[:, at : at + wide] = gat[2 * (us * (nz // 2) + j) + cc]
        at = pl.ds(pl.multiple_of(us * WIDTH, WIDTH), WIDTH)
        va[:, h * WIDTH : (h + 1) * WIDTH] = vgat[cc, :, at]


def restore(n, flags, *operands):
    vmem = pl.BlockSpec(memory_space=pltpu.VMEM)
    hw = KV_HEADS * WIDTH
    return pl.pallas_call(
        functools.partial(restore_kernel, n),
        in_specs=[pl.BlockSpec(memory_space=pltpu.SMEM)] + [vmem] * 4,
        out_specs=[vmem] * 5,
        out_shape=[
            jax.ShapeDtypeStruct((TOK, KV_HEADS * SPAN), BF16),
            jax.ShapeDtypeStruct((TOK, hw), BF16),
            jax.ShapeDtypeStruct((TOK, hw), BF16),
            jax.ShapeDtypeStruct((8, KV_HEADS * SPAN), F32),
            jax.ShapeDtypeStruct((8, hw), F32),
        ],
        compiler_params=pltpu.CompilerParams(vmem_limit_bytes=56 * 1024 * 1024),
        name="restore_heads",
    )(flags, *operands)


def position_tables(n):
    half = WIDTH // 2
    inv_freq = 10000.0 ** (-(np.arange(half) * 2.0) / WIDTH)
    angle = inv_freq[None, :, None] * np.arange(n * TOK).reshape(n // 2, 1, 2 * TOK)
    return np.stack([np.cos(angle), np.sin(angle)], axis=1).astype(np.float32)


def local(n, ndp, query, keys, values, out_grad, query_state, value_state, flags):
    tables = jnp.asarray(position_tables(n))
    places = main_call(
        n, ndp, flags, query[0], out_grad[0], keys[0], values[0], query_state[0].T, value_state[0].T, tables
    )
    qg, kg, vg, qa, va = restore(n, flags, *places)
    return qg[None], kg[None], vg[None], qa, va


def solution(mesh):
    split = P("dp", "ctx", None)
    return jax.shard_map(
        functools.partial(local, mesh.shape["ctx"], mesh.shape["dp"]),
        mesh=mesh,
        in_specs=(split,) * 6 + (P(),),
        out_specs=(split, split, split, P(), P()),
        check_vma=False,
    )
```
